768 devices in a mesh: dp: 48 (over y_hi, z, core), tensor: 16 (over y_lo, x).
Axes of the slice: x: 4, y: 8 (y_hi: 2, y_lo: 4; y = y_hi * 4 + y_lo), z: 12, core: 2. Of those that a mesh axis runs over, the one named last changes fastest.
Arguments:
- patches: bfloat16 [12288, 3072], P('dp', 'tensor'), may hold values from -6 to 6
- keep_order: int32 [48, 256], P('dp'), may hold values from 0 to 255, each once within a row
- keep_count: int32 [48], P('dp'), may hold values from 1 to 192, 6144 in all
- ln_gain: float32 [3072], replicated, may hold values from 0.1 to 1.9
- w_in: bfloat16 [3072, 12288], P('dp', 'tensor'), may hold values from -0.109375 to 0.109375
- cotangent: bfloat16 [12288, 12288], P('dp', 'tensor'), may hold values from -6 to 6
Outputs:
- hidden: bfloat16 [12288, 12288], P('dp', 'tensor')
- grad_patches: bfloat16 [12288, 3072], P('dp', 'tensor')
- w_grad: float32 [3072, 12288], P('dp', 'tensor')
The draws below stay inside these ranges and needn't reach their ends.
Inputs may be any that keep to these rules, and one draw needn't show every extreme that they name: Each row holds every patch number once; image i keeps the patches keep_order[i, 0] to keep_order[i, keep_count[i] - 1]. `keep_count`: the counts of all images add up to 6144; some image keeps exactly 192.
All inputs are finite; a program needn't handle non-finite values. No bound on the sum of `keep_count` on one device may be relied on, other than what follows from the above.
Results may differ from the reference program's by a relative error of at most 0.024.
Values may be sent and summed in bfloat16 or wider, within the bound.
No kernel may reach another device: no remote copies, remote signals or barrier semaphores. Data moves between devices by JAX's collectives and lax.ppermute only.
A program may use at most 64 MiB of HBM per device.

```python
import math
import jax
import jax.numpy as jnp
import numpy as np
from jax import lax

D = 3072
FF = 12288
PATCHES = 256
KMOST = 192
IMAGES = 48
ROWS = 12288
KEPT = 6144
N_TENSOR = 16


def shard_levels(key, dims, cuts, low, high):
    loudness = 1.0
    for axis_at, shards_of in cuts:
        steps = jax.random.uniform(jax.random.fold_in(jax.random.fold_in(key, 6), axis_at), (shards_of,), jnp.float32, low / len(cuts), high / len(cuts))
        loudness = loudness * jnp.repeat(jnp.exp(steps), dims[axis_at] // shards_of).reshape((-1,) + (1,) * (len(dims) - 1 - axis_at))
    return loudness


def length_profile(number_of, total, reach, slope):
    portions = [(1 << 20) // math.isqrt(grade ** slope) + 1 for grade in range(2, number_of + 1)]
    spare, holding = total - reach - (number_of - 1), [1] * (number_of - 1)
    while spare > 0:
        candidates = [i for i in range(number_of - 1) if holding[i] < reach]
        mass, left = sum([portions[i] for i in candidates]), spare
        for i in candidates:
            more = min(reach - holding[i], max(1, left * portions[i] // mass), spare)
            holding[i] = holding[i] + more
            spare = spare - more
    return np.array([reach] + holding)


def uneven(own_key, number_of, total, reach, slope):
    if number_of == 2:
        one = jax.random.randint(own_key, (), max(1, total - reach), min(reach, total - 1) + 1)
        return jnp.stack([one, total - one])
    tallies = jnp.asarray(length_profile(number_of, total, reach, slope), jnp.int32)
    pairs = (number_of - 1) // 2
    donor, taker = tallies[1:1 + 2 * pairs:2], tallies[2:2 + 2 * pairs:2]
    margin = jnp.minimum(donor - 1, reach - taker)
    passed = jax.random.randint(jax.random.fold_in(own_key, 1), (pairs,), 0, 1 << 20) % (margin + 1)
    tallies = tallies.at[1:1 + 2 * pairs:2].set(donor - passed).at[2:2 + 2 * pairs:2].set(taker + passed)
    return tallies[jax.random.permutation(jax.random.fold_in(own_key, 2), number_of)]


def normal_values(rng, extent, width, reach, pieces=(), kind=jnp.bfloat16):
    entries = jax.random.normal(rng, extent, jnp.float32) * width
    if len(pieces) > 0:
        entries = shard_levels(rng, extent, pieces, -0.22, 0.18) * entries
    return jnp.clip(entries, min=-reach, max=reach).astype(kind)


def setup_inputs(seed: int = 0) -> dict:
    seeds = jax.random.split(jax.random.key(seed), 7)
    patches = normal_values(seeds[0], (ROWS, D), 1.0, 6.0, ((0, 48), (1, 16)))
    keep_order = jax.vmap(lambda own: jax.random.permutation(own, PATCHES))(jax.random.split(seeds[1], IMAGES)).reshape((IMAGES, PATCHES)).astype(jnp.int32)
    keep_count = uneven(seeds[2], IMAGES, KEPT, KMOST, 2).astype(jnp.int32)
    ln_gain = jnp.clip(1.0 + 0.18 * jax.random.normal(seeds[3], (D,), jnp.float32), 0.1, 1.9)
    w_in = normal_values(seeds[4], (D, FF), D ** -0.5, 0.109375, ((0, 48), (1, 16)))
    cotangent = normal_values(seeds[5], (ROWS, FF), 1.0, 6.0, ((0, 48), (1, 16)))
    return {"patches": patches, "keep_order": keep_order, "keep_count": keep_count, "ln_gain": ln_gain, "w_in": w_in, "cotangent": cotangent}


def gelu_pair(pre_act):
    normal_cdf = 0.5 * (1.0 + lax.erf(pre_act * 0.7071067811865476))
    density = jnp.exp(-0.5 * pre_act * pre_act) * 0.3989422804014327
    return (pre_act * normal_cdf, normal_cdf + pre_act * density)

def reference(patches, keep_order, keep_count, ln_gain, w_in, cotangent):
    image_count = keep_order.shape[0]
    positions = jnp.broadcast_to(jnp.arange(PATCHES, dtype=jnp.int32)[None, :], (image_count, PATCHES))
    image_ids = jnp.broadcast_to(jnp.arange(image_count, dtype=jnp.int32)[:, None], (image_count, PATCHES))
    order_rank = jnp.zeros((image_count, PATCHES), jnp.int32).at[image_ids, keep_order].set(positions)
    keep_mask = (order_rank < keep_count[:, None]).reshape(-1)
    kept_rows = jnp.nonzero(keep_mask, size=KEPT, fill_value=0)[0].astype(jnp.int32)
    row_x = patches[kept_rows].astype(jnp.float32)
    row_mean = lax.optimization_barrier(jnp.mean(row_x, axis=1, keepdims=True))
    centered = row_x - row_mean
    row_var = lax.optimization_barrier(jnp.mean(centered * centered, axis=1, keepdims=True))
    inv_std = lax.rsqrt(row_var + 1e-06)
    normal_x = centered * inv_std
    normed = (normal_x * ln_gain[None, :]).astype(jnp.bfloat16)
    pre_act = jnp.dot(normed, w_in, preferred_element_type=jnp.float32)
    act_value, act_slope = gelu_pair(pre_act)
    hidden_rows = act_value.astype(jnp.bfloat16)
    cot_rows = cotangent[kept_rows].astype(jnp.float32)
    pre_grad = (cot_rows * act_slope).astype(jnp.bfloat16)
    block_size = FF // N_TENSOR
    normed_grad = jnp.zeros((KEPT, D), jnp.float32)
    for block_id in range(N_TENSOR):
        lower = block_id * block_size
        upper = lower + block_size
        part_sum = jnp.dot(pre_grad[:, lower:upper], w_in[:, lower:upper].T, preferred_element_type=jnp.float32)
        part_sum = lax.optimization_barrier(part_sum.astype(jnp.bfloat16))
        normed_grad = normed_grad + part_sum.astype(jnp.float32)
    scaled = normed_grad * ln_gain[None, :]
    first_mean = lax.optimization_barrier(jnp.mean(scaled, axis=1, keepdims=True))
    second_mean = lax.optimization_barrier(jnp.mean(scaled * normal_x, axis=1, keepdims=True))
    grad_rows = (inv_std * (scaled - first_mean - normal_x * second_mean)).astype(jnp.bfloat16)
    hidden = jnp.zeros((ROWS, FF), jnp.bfloat16).at[kept_rows].set(hidden_rows)
    grad_patches = jnp.zeros((ROWS, D), jnp.bfloat16).at[kept_rows].set(grad_rows)
    w_grad = lax.dot_general(normed, pre_grad, (((0,), (0,)), ((), ())), preferred_element_type=jnp.float32)
    return (hidden, grad_patches, w_grad)
```

```python
import jax
import jax.numpy as jnp
from jax import lax
from jax.sharding import Mesh, PartitionSpec as P

KMOST = 192
YH, Z, CORE, YL, X = 2, 12, 2, 4, 4
PIECES = 16


def gelu_pair(pre_act):
    normal_cdf = 0.5 * (1.0 + lax.erf(pre_act * 0.7071067811865476))
    density = jnp.exp(-0.5 * pre_act * pre_act) * 0.3989422804014327
    return (pre_act * normal_cdf, normal_cdf + pre_act * density)


def pieces_of(sums):
    high = lax.reduce_precision(sums, 8, 7)
    rest = sums - high
    middle = lax.reduce_precision(rest, 8, 7)
    low = rest - middle
    parts = jnp.concatenate([high, middle, low], axis=-2).astype(jnp.bfloat16)
    pad = [(0, 0)] * (sums.ndim - 2) + [(0, PIECES - 6), (0, 0)]
    return jnp.pad(parts, pad)


def sums_of(parts):
    total = jnp.sum(parts[:, :6].astype(jnp.float32), axis=0)
    return total[0:2] + total[2:4] + total[4:6]


def per_device(patches, keep_order, keep_count, ln_gain, w_in, cotangent):
    own_rows, col_width = patches.shape
    depth, ff_width = w_in.shape
    width = ln_gain.shape[0]
    half = width // CORE
    core = lax.axis_index("core")
    bf16, f32 = jnp.bfloat16, jnp.float32

    with jax.named_scope("weight_gather"):
        pair_weight = lax.all_gather(w_in, "yh", axis=0, tiled=True)
        weight = lax.all_gather(pair_weight, "z", axis=0, tiled=True)

    slot_ids = jnp.arange(KMOST, dtype=jnp.int32)
    row_ids = jnp.arange(own_rows, dtype=jnp.int32)
    slot_row = jnp.where(slot_ids < keep_count[0], keep_order[0, :KMOST], -1)
    select = (slot_row[:, None] == row_ids[None, :]).astype(bf16)

    with jax.named_scope("rows_gather"):
        own_x = lax.dot_general(
            patches, select, (((0,), (1,)), ((), ())), preferred_element_type=f32
        ).astype(bf16)
        block_x = lax.all_gather(own_x, "x", axis=0, tiled=True)
        blocks = block_x.shape[0] // (CORE * depth)
        by_core = block_x.reshape(blocks, CORE, depth, KMOST).transpose(1, 0, 2, 3)
        pair_x = lax.all_to_all(
            by_core.reshape(CORE, blocks * depth, KMOST), "core", split_axis=0, concat_axis=0, tiled=True
        )
        pair_x = jnp.concatenate([pair_x[0], pair_x[1]], axis=1)
        rows = pair_x.shape[1]
        cut = pair_x.shape[0] // 2
        parts = [lax.all_gather(pair_x[i * cut : (i + 1) * cut], "yl", axis=0, tiled=True) for i in range(2)]
        row_x = jnp.stack([p.reshape(YH, 2, blocks // 2, depth, rows) for p in parts])
        row_x = row_x.transpose(2, 0, 3, 1, 4, 5).reshape(half, rows)

    with jax.named_scope("row_moments"):
        x32 = row_x.astype(f32)
        part_mean = jnp.mean(x32, axis=0)
        part_square = jnp.sum(jnp.square(x32 - part_mean[None, :]), axis=0)
        both = lax.all_gather(jnp.stack([part_mean, part_square]), "core", axis=0)
        row_mean = 0.5 * (both[0, 0] + both[1, 0])
        apart = both[0, 0] - both[1, 0]
        row_var = (both[0, 1] + both[1, 1] + apart * apart * (0.5 * half)) / width
        inv_std = lax.rsqrt(row_var + 1e-06)
        gain = ln_gain.reshape(YH, Z, CORE, depth)
        gain = lax.dynamic_index_in_dim(gain, core, 2, keepdims=False)
        gain = gain.transpose(1, 0, 2).reshape(half)
        normal_x = (x32 - row_mean[None, :]) * inv_std[None, :]
        normed = (normal_x * gain[:, None]).astype(bf16)

    with jax.named_scope("forward"):
        rows_cot = jnp.dot(select, cotangent, preferred_element_type=f32)
        part_act = lax.dot_general(normed, weight, (((0,), (0,)), ((), ())), preferred_element_type=f32)
        part_act = lax.all_to_all(
            part_act.reshape(CORE, KMOST, ff_width), "core", split_axis=0, concat_axis=0, tiled=True
        )
        act_value, act_slope = gelu_pair(part_act[0] + part_act[1])
        pre_grad = (rows_cot * act_slope).astype(bf16)
        pair_grad = lax.all_gather(pre_grad, "core", axis=0, tiled=True)

    with jax.named_scope("weight_grad"):
        part_w = jnp.dot(normed, pair_grad, preferred_element_type=f32).astype(bf16)
        part_w, pair_grad = lax.optimization_barrier((part_w, pair_grad))
        pair_w = lax.psum_scatter(part_w, "z", scatter_dimension=0, tiled=True)

    with jax.named_scope("rows_grad"):
        part_x = lax.dot_general(weight, pair_grad, (((1,), (1,)), ((), ())), preferred_element_type=f32)
        part_x = part_x.astype(bf16)
        scaled = part_x.astype(f32) * gain[:, None]
        sums = jnp.stack([jnp.sum(scaled, axis=0), jnp.sum(scaled * normal_x, axis=0)])
        by_yl = part_x.reshape(2, blocks, YH, depth, rows).transpose(2, 0, 1, 3, 4)
        by_yl = by_yl.reshape(YL, blocks * depth, rows)
        extra = jnp.broadcast_to(pieces_of(sums)[None], (YL, PIECES, rows))
        got = lax.all_to_all(
            jnp.concatenate([by_yl, extra], axis=1), "yl", split_axis=0, concat_axis=0, tiled=True
        )
        sums = sums_of(got[:, -PIECES:])
        grad = jnp.sum(got[:, :-PIECES].astype(f32), axis=0).astype(bf16)
        grad = jnp.concatenate([grad, pieces_of(sums)], axis=0)
        by_core = jnp.stack([grad[:, :KMOST], grad[:, KMOST:]])
        got = lax.all_to_all(by_core, "core", split_axis=0, concat_axis=0, tiled=True)
        sums = sums_of(got[:, -PIECES:])
        grad = got[:, :-PIECES].reshape(CORE, blocks, depth, KMOST).transpose(1, 0, 2, 3)
        by_x = grad.reshape(X, col_width, KMOST)
        extra = jnp.broadcast_to(pieces_of(sums)[None], (X, PIECES, KMOST))
        got = lax.all_to_all(
            jnp.concatenate([by_x, extra], axis=1), "x", split_axis=0, concat_axis=0, tiled=True
        )
        sums = sums_of(got[:, -PIECES:])
        share_grad = jnp.sum(got[:, :-PIECES].astype(f32), axis=0)

    with jax.named_scope("rows_out"):
        col_start = (lax.axis_index("yl") * X + lax.axis_index("x")) * col_width
        share_gain = lax.dynamic_slice_in_dim(ln_gain, col_start, col_width, 0)
        own_mean = lax.dynamic_slice_in_dim(row_mean, core * KMOST, KMOST, 0)
        own_inv = lax.dynamic_slice_in_dim(inv_std, core * KMOST, KMOST, 0)
        share_x = (own_x.astype(f32) - own_mean[None, :]) * own_inv[None, :]
        scaled = share_grad * share_gain[:, None]
        means = sums / width
        grad_rows = own_inv[None, :] * (scaled - means[0:1] - share_x * means[1:2])
        grad_patches = lax.dot_general(
            select, grad_rows.astype(bf16), (((0,), (1,)), ((), ())), preferred_element_type=f32
        ).astype(bf16)
        hidden = lax.dot_general(
            select, act_value.astype(bf16), (((0,), (0,)), ((), ())), preferred_element_type=f32
        ).astype(bf16)

    with jax.named_scope("weight_out"):
        yh = lax.axis_index("yh")
        kept_w = lax.dynamic_slice_in_dim(pair_w, yh * depth, depth, 0)
        sent_w = lax.dynamic_slice_in_dim(pair_w, (1 - yh) * depth, depth, 0)
        met_w = lax.ppermute(sent_w, "yh", [(0, 1), (1, 0)])
        w_grad = kept_w.astype(f32) + met_w.astype(f32)
    return (hidden, grad_patches, w_grad)


def solution(mesh):
    fine = Mesh(mesh.devices.reshape(YH, Z, CORE, YL, X), ("yh", "z", "core", "yl", "x"))
    dp, tensor = ("yh", "z", "core"), ("yl", "x")
    both = P(dp, tensor)
    return jax.shard_map(
        per_device,
        mesh=fine,
        in_specs=(both, P(dp, None), P(dp), P(), both, both),
        out_specs=(both, both, both),
        check_vma=False,
    )
```

```python
import jax
import jax.numpy as jnp
from jax import lax
from jax.sharding import Mesh, PartitionSpec as P

KMOST = 192
YH, Z, CORE, YL, X = 2, 12, 2, 4, 4
PIECES = 16


def gelu_pair(pre_act):
    normal_cdf = 0.5 * (1.0 + lax.erf(pre_act * 0.7071067811865476))
    density = jnp.exp(-0.5 * pre_act * pre_act) * 0.3989422804014327
    return (pre_act * normal_cdf, normal_cdf + pre_act * density)


def pieces_of(sums):
    high = lax.reduce_precision(sums, 8, 7)
    rest = sums - high
    middle = lax.reduce_precision(rest, 8, 7)
    low = rest - middle
    parts = jnp.concatenate([high, middle, low], axis=-2).astype(jnp.bfloat16)
    pad = [(0, 0)] * (sums.ndim - 2) + [(0, PIECES - 6), (0, 0)]
    return jnp.pad(parts, pad)


def sums_of(parts):
    total = jnp.sum(parts[:, :6].astype(jnp.float32), axis=0)
    return total[0:2] + total[2:4] + total[4:6]


def per_device(patches, keep_order, keep_count, ln_gain, w_in, cotangent):
    own_rows, col_width = patches.shape
    depth, ff_width = w_in.shape
    width = ln_gain.shape[0]
    half = width // CORE
    core = lax.axis_index("core")
    bf16, f32 = jnp.bfloat16, jnp.float32

    with jax.named_scope("weight_gather"):
        pair_weight = lax.all_gather(w_in, "yh", axis=0, tiled=True)
        weight = lax.all_gather(pair_weight, "z", axis=0, tiled=True)

    slot_ids = jnp.arange(KMOST, dtype=jnp.int32)
    row_ids = jnp.arange(own_rows, dtype=jnp.int32)
    slot_row = jnp.where(slot_ids < keep_count[0], keep_order[0, :KMOST], -1)
    select = (slot_row[:, None] == row_ids[None, :]).astype(bf16)

    with jax.named_scope("rows_gather"):
        own_x = lax.dot_general(
            patches, select, (((0,), (1,)), ((), ())), preferred_element_type=f32
        ).astype(bf16)
        block_x = lax.all_gather(own_x, "x", axis=0, tiled=True)
        blocks = block_x.shape[0] // (CORE * depth)
        by_core = block_x.reshape(blocks, CORE, depth, KMOST).transpose(1, 0, 2, 3)
        pair_x = lax.all_to_all(
            by_core.reshape(CORE, blocks * depth, KMOST), "core", split_axis=0, concat_axis=0, tiled=True
        )
        pair_x = jnp.concatenate([pair_x[0], pair_x[1]], axis=1)
        rows = pair_x.shape[1]
        cut = pair_x.shape[0] // 2
        parts = [lax.all_gather(pair_x[i * cut : (i + 1) * cut], "yl", axis=0, tiled=True) for i in range(2)]
        row_x = jnp.stack([p.reshape(YH, 2, blocks // 2, depth, rows) for p in parts])
        row_x = row_x.transpose(2, 0, 3, 1, 4, 5).reshape(half, rows)

    with jax.named_scope("row_moments"):
        x32 = row_x.astype(f32)
        part_mean = jnp.mean(x32, axis=0)
        part_square = jnp.sum(jnp.square(x32 - part_mean[None, :]), axis=0)
        both = lax.all_gather(jnp.stack([part_mean, part_square]), "core", axis=0)
        row_mean = 0.5 * (both[0, 0] + both[1, 0])
        apart = both[0, 0] - both[1, 0]
        row_var = (both[0, 1] + both[1, 1] + apart * apart * (0.5 * half)) / width
        inv_std = lax.rsqrt(row_var + 1e-06)
        gain = ln_gain.reshape(YH, Z, CORE, depth)
        gain = lax.dynamic_index_in_dim(gain, core, 2, keepdims=False)
        gain = gain.transpose(1, 0, 2).reshape(half)
        normal_x = (x32 - row_mean[None, :]) * inv_std[None, :]
        normed = (normal_x * gain[:, None]).astype(bf16)

    with jax.named_scope("forward"):
        rows_cot = jnp.dot(select, cotangent, preferred_element_type=f32)
        part_act = lax.dot_general(normed, weight, (((0,), (0,)), ((), ())), preferred_element_type=f32)
        part_act = lax.all_to_all(
            part_act.reshape(CORE, KMOST, ff_width), "core", split_axis=0, concat_axis=0, tiled=True
        )
        act_value, act_slope = gelu_pair(part_act[0] + part_act[1])
        pre_grad = (rows_cot * act_slope).astype(bf16)
        pair_grad = lax.all_gather(pre_grad, "core", axis=0, tiled=True)

    with jax.named_scope("weight_grad"):
        part_w = jnp.dot(normed, pair_grad, preferred_element_type=f32).astype(bf16)
        part_w, pair_grad = lax.optimization_barrier((part_w, pair_grad))
        pair_w = lax.psum_scatter(part_w, "z", scatter_dimension=0, tiled=True)

    def rows_grad(pair_grad):
        part_x = lax.dot_general(weight, pair_grad, (((1,), (1,)), ((), ())), preferred_element_type=f32)
        part_x = part_x.astype(bf16)
        scaled = part_x.astype(f32) * gain[:, None]
        sums = jnp.stack([jnp.sum(scaled, axis=0), jnp.sum(scaled * normal_x, axis=0)])
        by_yl = part_x.reshape(2, blocks, YH, depth, rows).transpose(2, 0, 1, 3, 4)
        by_yl = by_yl.reshape(YL, blocks * depth, rows)
        extra = jnp.broadcast_to(pieces_of(sums)[None], (YL, PIECES, rows))
        got = lax.all_to_all(
            jnp.concatenate([by_yl, extra], axis=1), "yl", split_axis=0, concat_axis=0, tiled=True
        )
        sums = sums_of(got[:, -PIECES:])
        grad = jnp.sum(got[:, :-PIECES].astype(f32), axis=0).astype(bf16)
        grad = jnp.concatenate([grad, pieces_of(sums)], axis=0)
        by_core = jnp.stack([grad[:, :KMOST], grad[:, KMOST:]])
        got = lax.all_to_all(by_core, "core", split_axis=0, concat_axis=0, tiled=True)
        sums = sums_of(got[:, -PIECES:])
        grad = got[:, :-PIECES].reshape(CORE, blocks, depth, KMOST).transpose(1, 0, 2, 3)
        by_x = grad.reshape(X, col_width, KMOST)
        extra = jnp.broadcast_to(pieces_of(sums)[None], (X, PIECES, KMOST))
        got = lax.all_to_all(
            jnp.concatenate([by_x, extra], axis=1), "x", split_axis=0, concat_axis=0, tiled=True
        )
        sums = sums_of(got[:, -PIECES:])
        share_grad = jnp.sum(got[:, :-PIECES].astype(f32), axis=0)


        return sums, share_grad

    with jax.named_scope("rows_grad"):
        sums, share_grad = lax.cond(
            keep_count[0] > 0,
            rows_grad,
            lambda g: (jnp.zeros((2, KMOST), f32), jnp.zeros((col_width, KMOST), f32)),
            pair_grad,
        )

    with jax.named_scope("rows_out"):
        col_start = (lax.axis_index("yl") * X + lax.axis_index("x")) * col_width
        share_gain = lax.dynamic_slice_in_dim(ln_gain, col_start, col_width, 0)
        own_mean = lax.dynamic_slice_in_dim(row_mean, core * KMOST, KMOST, 0)
        own_inv = lax.dynamic_slice_in_dim(inv_std, core * KMOST, KMOST, 0)
        share_x = (own_x.astype(f32) - own_mean[None, :]) * own_inv[None, :]
        scaled = share_grad * share_gain[:, None]
        means = sums / width
        grad_rows = own_inv[None, :] * (scaled - means[0:1] - share_x * means[1:2])
        grad_patches = lax.dot_general(
            select, grad_rows.astype(bf16), (((0,), (1,)), ((), ())), preferred_element_type=f32
        ).astype(bf16)
        hidden = lax.dot_general(
            select, act_value.astype(bf16), (((0,), (0,)), ((), ())), preferred_element_type=f32
        ).astype(bf16)

    with jax.named_scope("weight_out"):
        yh = lax.axis_index("yh")
        kept_w = lax.dynamic_slice_in_dim(pair_w, yh * depth, depth, 0)
        sent_w = lax.dynamic_slice_in_dim(pair_w, (1 - yh) * depth, depth, 0)
        met_w = lax.ppermute(sent_w, "yh", [(0, 1), (1, 0)])
        w_grad = kept_w.astype(f32) + met_w.astype(f32)
    return (hidden, grad_patches, w_grad)


def solution(mesh):
    fine = Mesh(mesh.devices.reshape(YH, Z, CORE, YL, X), ("yh", "z", "core", "yl", "x"))
    dp, tensor = ("yh", "z", "core"), ("yl", "x")
    both = P(dp, tensor)
    return jax.shard_map(
        per_device,
        mesh=fine,
        in_specs=(both, P(dp, None), P(dp), P(), both, both),
        out_specs=(both, both, both),
        check_vma=False,
    )
```

```python
import jax
import jax.numpy as jnp
from jax import lax
from jax.sharding import Mesh, PartitionSpec as P

KMOST = 192
YH, Z, CORE, YL, X = 2, 12, 2, 4, 4
PIECES = 16


def gelu_pair(pre_act):
    normal_cdf = 0.5 * (1.0 + lax.erf(pre_act * 0.7071067811865476))
    density = jnp.exp(-0.5 * pre_act * pre_act) * 0.3989422804014327
    return (pre_act * normal_cdf, normal_cdf + pre_act * density)


def pieces_of(sums):
    high = lax.reduce_precision(sums, 8, 7)
    rest = sums - high
    middle = lax.reduce_precision(rest, 8, 7)
    low = rest - middle
    parts = jnp.concatenate([high, middle, low], axis=-2).astype(jnp.bfloat16)
    pad = [(0, 0)] * (sums.ndim - 2) + [(0, PIECES - 6), (0, 0)]
    return jnp.pad(parts, pad)


def sums_of(parts):
    total = jnp.sum(parts[:, :6].astype(jnp.float32), axis=0)
    return total[0:2] + total[2:4] + total[4:6]


def gather_weight(shard):
    f32 = jnp.float32
    count, ff_width = shard.shape
    shard = shard.astype(f32)
    top = jnp.maximum(jnp.max(jnp.abs(shard)), 1e-33)
    scale = lax.reduce_precision(16384.0 / top, 8, 0)
    power = jnp.broadcast_to(jnp.round(jnp.log2(scale)), (16, ff_width))
    sent = jnp.concatenate([shard * scale, power]).astype(jnp.float16)
    got = lax.all_gather(sent, "z", axis=0)
    shrink = lax.reduce_precision(jnp.exp2(-got[:, count : count + 1].astype(f32)), 8, 0)
    weight = (got[:, :count].astype(f32) * shrink).astype(jnp.bfloat16)
    return weight.reshape(-1, ff_width)


def per_device(patches, keep_order, keep_count, ln_gain, w_in, cotangent):
    own_rows, col_width = patches.shape
    depth, ff_width = w_in.shape
    width = ln_gain.shape[0]
    half = width // CORE
    core = lax.axis_index("core")
    bf16, f32 = jnp.bfloat16, jnp.float32

    slot_ids = jnp.arange(KMOST, dtype=jnp.int32)
    row_ids = jnp.arange(own_rows, dtype=jnp.int32)
    slot_row = jnp.where(slot_ids < keep_count[0], keep_order[0, :KMOST], -1)
    select = (slot_row[:, None] == row_ids[None, :]).astype(bf16)
    blocks = Z // 2
    rows = CORE * KMOST

    with jax.named_scope("weight_pair"):
        met_weight = lax.ppermute(w_in, "yh", [(0, 1), (1, 0)])

    with jax.named_scope("rows_gather"):
        own_x = lax.dot_general(
            patches, select, (((0,), (1,)), ((), ())), preferred_element_type=f32
        ).astype(bf16)
        pair_x = lax.all_gather(own_x, "core", axis=0)
        pair_x = jnp.concatenate([pair_x[0], pair_x[1]], axis=1).reshape(3, depth, rows)
        two = (lax.axis_index("x") + core) % 2 == 0
        runs = jnp.stack([jnp.where(two, pair_x[0], pair_x[1]), pair_x[2]])
        runs = jnp.broadcast_to(runs.reshape(1, 2 * depth, rows), (YL * X, 2 * depth, rows))
        got_x = lax.all_to_all(runs, ("yl", "x"), split_axis=0, concat_axis=0, tiled=True)

    with jax.named_scope("weight_gather"):
        first = lax.axis_index("yh") == 0
        pair_weight = jnp.concatenate([jnp.where(first, w_in, met_weight), jnp.where(first, met_weight, w_in)])
        weight = gather_weight(pair_weight)

    with jax.named_scope("rows_order"):
        got_x = got_x.reshape(YL * X // 2, 4, depth, rows)
        low = core == 0
        row_x = jnp.stack(
            [got_x[:, 0], jnp.where(low, got_x[:, 1], got_x[:, 2]), jnp.where(low, got_x[:, 2], got_x[:, 3])], axis=1
        )
        row_x = row_x.reshape(YH, Z, depth, rows).transpose(1, 0, 2, 3).reshape(half, rows)

    with jax.named_scope("row_moments"):
        x32 = row_x.astype(f32)
        part_mean = jnp.mean(x32, axis=0)
        part_square = jnp.sum(jnp.square(x32 - part_mean[None, :]), axis=0)
        both = lax.all_gather(jnp.stack([part_mean, part_square]), "core", axis=0)
        row_mean = 0.5 * (both[0, 0] + both[1, 0])
        apart = both[0, 0] - both[1, 0]
        row_var = (both[0, 1] + both[1, 1] + apart * apart * (0.5 * half)) / width
        inv_std = lax.rsqrt(row_var + 1e-06)
        gain = ln_gain.reshape(YH, Z, CORE, depth)
        gain = lax.dynamic_index_in_dim(gain, core, 2, keepdims=False)
        gain = gain.transpose(1, 0, 2).reshape(half)
        normal_x = (x32 - row_mean[None, :]) * inv_std[None, :]
        normed = (normal_x * gain[:, None]).astype(bf16)

    with jax.named_scope("forward"):
        rows_cot = jnp.dot(select, cotangent, preferred_element_type=f32)
        part_act = lax.dot_general(normed, weight, (((0,), (0,)), ((), ())), preferred_element_type=f32)
        part_act = lax.all_to_all(
            part_act.reshape(CORE, KMOST, ff_width), "core", split_axis=0, concat_axis=0, tiled=True
        )
        act_value, act_slope = gelu_pair(part_act[0] + part_act[1])
        pre_grad = (rows_cot * act_slope).astype(bf16)
        pair_grad = lax.all_gather(pre_grad, "core", axis=0, tiled=True)

    with jax.named_scope("weight_grad"):
        part_w = jnp.dot(normed, pair_grad, preferred_element_type=f32).astype(bf16)
        part_w, pair_grad = lax.optimization_barrier((part_w, pair_grad))
        pair_w = lax.psum_scatter(part_w, "z", scatter_dimension=0, tiled=True)

    def rows_grad(pair_grad):
        part_x = lax.dot_general(weight, pair_grad, (((1,), (1,)), ((), ())), preferred_element_type=f32)
        part_x = part_x.astype(bf16)
        scaled = part_x.astype(f32) * gain[:, None]
        sums = jnp.stack([jnp.sum(scaled, axis=0), jnp.sum(scaled * normal_x, axis=0)])
        by_yl = part_x.reshape(2, blocks, YH, depth, rows).transpose(2, 0, 1, 3, 4)
        by_yl = by_yl.reshape(YL, blocks * depth, rows)
        extra = jnp.broadcast_to(pieces_of(sums)[None], (YL, PIECES, rows))
        got = lax.all_to_all(
            jnp.concatenate([by_yl, extra], axis=1), "yl", split_axis=0, concat_axis=0, tiled=True
        )
        sums = sums_of(got[:, -PIECES:])
        grad = jnp.sum(got[:, :-PIECES].astype(f32), axis=0).astype(bf16)
        grad = jnp.concatenate([grad, pieces_of(sums)], axis=0)
        by_core = jnp.stack([grad[:, :KMOST], grad[:, KMOST:]])
        got = lax.all_to_all(by_core, "core", split_axis=0, concat_axis=0, tiled=True)
        sums = sums_of(got[:, -PIECES:])
        grad = got[:, :-PIECES].reshape(CORE, blocks, depth, KMOST).transpose(1, 0, 2, 3)
        by_x = grad.reshape(X, col_width, KMOST)
        extra = jnp.broadcast_to(pieces_of(sums)[None], (X, PIECES, KMOST))
        got = lax.all_to_all(
            jnp.concatenate([by_x, extra], axis=1), "x", split_axis=0, concat_axis=0, tiled=True
        )
        sums = sums_of(got[:, -PIECES:])
        share_grad = jnp.sum(got[:, :-PIECES].astype(f32), axis=0)


        return sums, share_grad

    with jax.named_scope("rows_grad"):
        sums, share_grad = lax.cond(
            keep_count[0] > 0,
            rows_grad,
            lambda g: (jnp.zeros((2, KMOST), f32), jnp.zeros((col_width, KMOST), f32)),
            pair_grad,
        )

    with jax.named_scope("rows_out"):
        col_start = (lax.axis_index("yl") * X + lax.axis_index("x")) * col_width
        share_gain = lax.dynamic_slice_in_dim(ln_gain, col_start, col_width, 0)
        own_mean = lax.dynamic_slice_in_dim(row_mean, core * KMOST, KMOST, 0)
        own_inv = lax.dynamic_slice_in_dim(inv_std, core * KMOST, KMOST, 0)
        share_x = (own_x.astype(f32) - own_mean[None, :]) * own_inv[None, :]
        scaled = share_grad * share_gain[:, None]
        means = sums / width
        grad_rows = own_inv[None, :] * (scaled - means[0:1] - share_x * means[1:2])
        grad_patches = lax.dot_general(
            select, grad_rows.astype(bf16), (((0,), (1,)), ((), ())), preferred_element_type=f32
        ).astype(bf16)
        hidden = lax.dot_general(
            select, act_value.astype(bf16), (((0,), (0,)), ((), ())), preferred_element_type=f32
        ).astype(bf16)

    with jax.named_scope("weight_out"):
        yh = lax.axis_index("yh")
        kept_w = lax.dynamic_slice_in_dim(pair_w, yh * depth, depth, 0)
        sent_w = lax.dynamic_slice_in_dim(pair_w, (1 - yh) * depth, depth, 0)
        met_w = lax.ppermute(sent_w, "yh", [(0, 1), (1, 0)])
        w_grad = kept_w.astype(f32) + met_w.astype(f32)
    return (hidden, grad_patches, w_grad)


def solution(mesh):
    fine = Mesh(mesh.devices.reshape(YH, Z, CORE, YL, X), ("yh", "z", "core", "yl", "x"))
    dp, tensor = ("yh", "z", "core"), ("yl", "x")
    both = P(dp, tensor)
    return jax.shard_map(
        per_device,
        mesh=fine,
        in_specs=(both, P(dp, None), P(dp), P(), both, both),
        out_specs=(both, both, both),
        check_vma=False,
    )
```

```python
import jax
import jax.numpy as jnp
from jax import lax
from jax.sharding import Mesh, PartitionSpec as P

KMOST = 192
YH, Z, CORE, YL, X = 2, 12, 2, 4, 4
PIECES = 16


def gelu_pair(pre_act):
    normal_cdf = 0.5 * (1.0 + lax.erf(pre_act * 0.7071067811865476))
    density = jnp.exp(-0.5 * pre_act * pre_act) * 0.3989422804014327
    return (pre_act * normal_cdf, normal_cdf + pre_act * density)


def pieces_of(sums):
    high = lax.reduce_precision(sums, 8, 7)
    rest = sums - high
    middle = lax.reduce_precision(rest, 8, 7)
    low = rest - middle
    parts = jnp.concatenate([high, middle, low], axis=-2).astype(jnp.bfloat16)
    pad = [(0, 0)] * (sums.ndim - 2) + [(0, PIECES - 6), (0, 0)]
    return jnp.pad(parts, pad)


def sums_of(parts):
    total = jnp.sum(parts[:, :6].astype(jnp.float32), axis=0)
    return total[0:2] + total[2:4] + total[4:6]


def gather_weight(shard):
    f32 = jnp.float32
    count, ff_width = shard.shape
    shard = shard.astype(f32)
    top = jnp.maximum(jnp.max(jnp.abs(shard)), 1e-33)
    scale = lax.reduce_precision(16384.0 / top, 8, 0)
    power = jnp.broadcast_to(jnp.round(jnp.log2(scale)), (16, ff_width))
    sent = jnp.concatenate([shard * scale, power]).astype(jnp.float16)
    got = lax.all_gather(sent, "z", axis=0)
    shrink = lax.reduce_precision(jnp.exp2(-got[:, count : count + 1].astype(f32)), 8, 0)
    weight = (got[:, :count].astype(f32) * shrink).astype(jnp.bfloat16)
    return weight.reshape(-1, ff_width)


def per_device(patches, keep_order, keep_count, ln_gain, w_in, cotangent):
    own_rows, col_width = patches.shape
    depth, ff_width = w_in.shape
    width = ln_gain.shape[0]
    half = width // CORE
    core = lax.axis_index("core")
    bf16, f32 = jnp.bfloat16, jnp.float32

    slot_ids = jnp.arange(KMOST, dtype=jnp.int32)
    row_ids = jnp.arange(own_rows, dtype=jnp.int32)
    slot_row = jnp.where(slot_ids < keep_count[0], keep_order[0, :KMOST], -1)
    select = (slot_row[:, None] == row_ids[None, :]).astype(bf16)
    blocks = Z // 2
    rows = CORE * KMOST

    with jax.named_scope("weight_pair"):
        met_weight = lax.ppermute(w_in, "yh", [(0, 1), (1, 0)])

    with jax.named_scope("rows_gather"):
        own_x = lax.dot_general(
            patches, select, (((0,), (1,)), ((), ())), preferred_element_type=f32
        ).astype(bf16)
        pair_x = lax.all_gather(own_x, "core", axis=0)
        pair_x = jnp.concatenate([pair_x[0], pair_x[1]], axis=1).reshape(3, depth, rows)
        two = (lax.axis_index("x") + core) % 2 == 0
        runs = jnp.stack([jnp.where(two, pair_x[0], pair_x[1]), pair_x[2]])
        runs, met_weight = lax.optimization_barrier((runs, met_weight))
        runs = jnp.broadcast_to(runs.reshape(1, 2 * depth, rows), (YL * X, 2 * depth, rows))
        got_x = lax.all_to_all(runs, ("yl", "x"), split_axis=0, concat_axis=0, tiled=True)

    with jax.named_scope("weight_gather"):
        first = lax.axis_index("yh") == 0
        pair_weight = jnp.concatenate([jnp.where(first, w_in, met_weight), jnp.where(first, met_weight, w_in)])
        weight = gather_weight(pair_weight)

    with jax.named_scope("rows_order"):
        got_x = got_x.reshape(YL * X // 2, 4, depth, rows)
        low = core == 0
        row_x = jnp.stack(
            [got_x[:, 0], jnp.where(low, got_x[:, 1], got_x[:, 2]), jnp.where(low, got_x[:, 2], got_x[:, 3])], axis=1
        )
        row_x = row_x.reshape(YH, Z, depth, rows).transpose(1, 0, 2, 3).reshape(half, rows)

    with jax.named_scope("row_moments"):
        x32 = row_x.astype(f32)
        part_mean = jnp.mean(x32, axis=0)
        part_square = jnp.sum(jnp.square(x32 - part_mean[None, :]), axis=0)
        both = lax.all_gather(jnp.stack([part_mean, part_square]), "core", axis=0)
        row_mean = 0.5 * (both[0, 0] + both[1, 0])
        apart = both[0, 0] - both[1, 0]
        row_var = (both[0, 1] + both[1, 1] + apart * apart * (0.5 * half)) / width
        inv_std = lax.rsqrt(row_var + 1e-06)
        gain = ln_gain.reshape(YH, Z, CORE, depth)
        gain = lax.dynamic_index_in_dim(gain, core, 2, keepdims=False)
        gain = gain.transpose(1, 0, 2).reshape(half)
        normal_x = (x32 - row_mean[None, :]) * inv_std[None, :]
        normed = (normal_x * gain[:, None]).astype(bf16)

    with jax.named_scope("forward"):
        rows_cot = jnp.dot(select, cotangent, preferred_element_type=f32)
        part_act = lax.dot_general(normed, weight, (((0,), (0,)), ((), ())), preferred_element_type=f32)
        part_act = lax.all_to_all(
            part_act.reshape(CORE, KMOST, ff_width), "core", split_axis=0, concat_axis=0, tiled=True
        )
        act_value, act_slope = gelu_pair(part_act[0] + part_act[1])
        pre_grad = (rows_cot * act_slope).astype(bf16)
        pair_grad = lax.all_gather(pre_grad, "core", axis=0, tiled=True)

    with jax.named_scope("weight_grad"):
        part_w = jnp.dot(normed, pair_grad, preferred_element_type=f32).astype(bf16)
        part_w, pair_grad = lax.optimization_barrier((part_w, pair_grad))
        pair_w = lax.psum_scatter(part_w, "z", scatter_dimension=0, tiled=True)

    def rows_grad(pair_grad):
        part_x = lax.dot_general(weight, pair_grad, (((1,), (1,)), ((), ())), preferred_element_type=f32)
        part_x = part_x.astype(bf16)
        scaled = part_x.astype(f32) * gain[:, None]
        sums = jnp.stack([jnp.sum(scaled, axis=0), jnp.sum(scaled * normal_x, axis=0)])
        by_yl = part_x.reshape(2, blocks, YH, depth, rows).transpose(2, 0, 1, 3, 4)
        by_yl = by_yl.reshape(YL, blocks * depth, rows)
        extra = jnp.broadcast_to(pieces_of(sums)[None], (YL, PIECES, rows))
        got = lax.all_to_all(
            jnp.concatenate([by_yl, extra], axis=1), "yl", split_axis=0, concat_axis=0, tiled=True
        )
        sums = sums_of(got[:, -PIECES:])
        grad = jnp.sum(got[:, :-PIECES].astype(f32), axis=0).astype(bf16)
        grad = jnp.concatenate([grad, pieces_of(sums)], axis=0)
        by_core = jnp.stack([grad[:, :KMOST], grad[:, KMOST:]])
        got = lax.all_to_all(by_core, "core", split_axis=0, concat_axis=0, tiled=True)
        sums = sums_of(got[:, -PIECES:])
        grad = got[:, :-PIECES].reshape(CORE, blocks, depth, KMOST).transpose(1, 0, 2, 3)
        by_x = grad.reshape(X, col_width, KMOST)
        extra = jnp.broadcast_to(pieces_of(sums)[None], (X, PIECES, KMOST))
        got = lax.all_to_all(
            jnp.concatenate([by_x, extra], axis=1), "x", split_axis=0, concat_axis=0, tiled=True
        )
        sums = sums_of(got[:, -PIECES:])
        share_grad = jnp.sum(got[:, :-PIECES].astype(f32), axis=0)


        return sums, share_grad

    with jax.named_scope("rows_grad"):
        sums, share_grad = lax.cond(
            keep_count[0] > 0,
            rows_grad,
            lambda g: (jnp.zeros((2, KMOST), f32), jnp.zeros((col_width, KMOST), f32)),
            pair_grad,
        )

    with jax.named_scope("rows_out"):
        col_start = (lax.axis_index("yl") * X + lax.axis_index("x")) * col_width
        share_gain = lax.dynamic_slice_in_dim(ln_gain, col_start, col_width, 0)
        own_mean = lax.dynamic_slice_in_dim(row_mean, core * KMOST, KMOST, 0)
        own_inv = lax.dynamic_slice_in_dim(inv_std, core * KMOST, KMOST, 0)
        share_x = (own_x.astype(f32) - own_mean[None, :]) * own_inv[None, :]
        scaled = share_grad * share_gain[:, None]
        means = sums / width
        grad_rows = own_inv[None, :] * (scaled - means[0:1] - share_x * means[1:2])
        grad_patches = lax.dot_general(
            select, grad_rows.astype(bf16), (((0,), (1,)), ((), ())), preferred_element_type=f32
        ).astype(bf16)
        hidden = lax.dot_general(
            select, act_value.astype(bf16), (((0,), (0,)), ((), ())), preferred_element_type=f32
        ).astype(bf16)

    with jax.named_scope("weight_out"):
        yh = lax.axis_index("yh")
        kept_w = lax.dynamic_slice_in_dim(pair_w, yh * depth, depth, 0)
        sent_w = lax.dynamic_slice_in_dim(pair_w, (1 - yh) * depth, depth, 0)
        met_w = lax.ppermute(sent_w, "yh", [(0, 1), (1, 0)])
        w_grad = kept_w.astype(f32) + met_w.astype(f32)
    return (hidden, grad_patches, w_grad)


def solution(mesh):
    fine = Mesh(mesh.devices.reshape(YH, Z, CORE, YL, X), ("yh", "z", "core", "yl", "x"))
    dp, tensor = ("yh", "z", "core"), ("yl", "x")
    both = P(dp, tensor)
    return jax.shard_map(
        per_device,
        mesh=fine,
        in_specs=(both, P(dp, None), P(dp), P(), both, both),
        out_specs=(both, both, both),
        check_vma=False,
    )
```

```python
import jax
import jax.numpy as jnp
from jax import lax
from jax.sharding import Mesh, PartitionSpec as P

KMOST = 192
YH, Z, CORE, YL, X = 2, 12, 2, 4, 4
PIECES = 16


def gelu_pair(pre_act):
    normal_cdf = 0.5 * (1.0 + lax.erf(pre_act * 0.7071067811865476))
    density = jnp.exp(-0.5 * pre_act * pre_act) * 0.3989422804014327
    return (pre_act * normal_cdf, normal_cdf + pre_act * density)


def pieces_of(sums):
    high = lax.reduce_precision(sums, 8, 7)
    rest = sums - high
    middle = lax.reduce_precision(rest, 8, 7)
    low = rest - middle
    parts = jnp.concatenate([high, middle, low], axis=-2).astype(jnp.bfloat16)
    pad = [(0, 0)] * (sums.ndim - 2) + [(0, PIECES - 6), (0, 0)]
    return jnp.pad(parts, pad)


def sums_of(parts):
    total = jnp.sum(parts[:, :6].astype(jnp.float32), axis=0)
    return total[0:2] + total[2:4] + total[4:6]


def per_device(patches, keep_order, keep_count, ln_gain, w_in, cotangent):
    own_rows, col_width = patches.shape
    depth, ff_width = w_in.shape
    width = ln_gain.shape[0]
    half = width // CORE
    core = lax.axis_index("core")
    bf16, f32 = jnp.bfloat16, jnp.float32

    slot_ids = jnp.arange(KMOST, dtype=jnp.int32)
    row_ids = jnp.arange(own_rows, dtype=jnp.int32)
    slot_row = jnp.where(slot_ids < keep_count[0], keep_order[0, :KMOST], -1)
    select = (slot_row[:, None] == row_ids[None, :]).astype(bf16)

    with jax.named_scope("weight_pair"):
        met_weight = lax.ppermute(w_in, "yh", [(0, 1), (1, 0)])

    with jax.named_scope("own_rows"):
        own_x = lax.dot_general(
            patches, select, (((0,), (1,)), ((), ())), preferred_element_type=f32
        ).astype(bf16)

    with jax.named_scope("weight_gather"):
        own_x, met_weight = lax.optimization_barrier((own_x, met_weight))
        first = lax.axis_index("yh") == 0
        pair_weight = jnp.concatenate([jnp.where(first, w_in, met_weight), jnp.where(first, met_weight, w_in)])
        weight = lax.all_gather(pair_weight, "z", axis=0, tiled=True)

    with jax.named_scope("rows_gather"):
        block_x = lax.all_gather(own_x, "x", axis=0, tiled=True)
        blocks = block_x.shape[0] // (CORE * depth)
        by_core = block_x.reshape(blocks, CORE, depth, KMOST).transpose(1, 0, 2, 3)
        pair_x = lax.all_to_all(
            by_core.reshape(CORE, blocks * depth, KMOST), "core", split_axis=0, concat_axis=0, tiled=True
        )
        pair_x = jnp.concatenate([pair_x[0], pair_x[1]], axis=1)
        rows = pair_x.shape[1]
        cut = pair_x.shape[0] // 2
        parts = [lax.all_gather(pair_x[i * cut : (i + 1) * cut], "yl", axis=0, tiled=True) for i in range(2)]
        row_x = jnp.stack([p.reshape(YH, 2, blocks // 2, depth, rows) for p in parts])
        row_x = row_x.transpose(2, 0, 3, 1, 4, 5).reshape(half, rows)

    with jax.named_scope("row_moments"):
        x32 = row_x.astype(f32)
        part_mean = jnp.mean(x32, axis=0)
        part_square = jnp.sum(jnp.square(x32 - part_mean[None, :]), axis=0)
        both = lax.all_gather(jnp.stack([part_mean, part_square]), "core", axis=0)
        row_mean = 0.5 * (both[0, 0] + both[1, 0])
        apart = both[0, 0] - both[1, 0]
        row_var = (both[0, 1] + both[1, 1] + apart * apart * (0.5 * half)) / width
        inv_std = lax.rsqrt(row_var + 1e-06)
        gain = ln_gain.reshape(YH, Z, CORE, depth)
        gain = lax.dynamic_index_in_dim(gain, core, 2, keepdims=False)
        gain = gain.transpose(1, 0, 2).reshape(half)
        normal_x = (x32 - row_mean[None, :]) * inv_std[None, :]
        normed = (normal_x * gain[:, None]).astype(bf16)

    with jax.named_scope("forward"):
        rows_cot = jnp.dot(select, cotangent, preferred_element_type=f32)
        part_act = lax.dot_general(normed, weight, (((0,), (0,)), ((), ())), preferred_element_type=f32)
        part_act = lax.all_to_all(
            part_act.reshape(CORE, KMOST, ff_width), "core", split_axis=0, concat_axis=0, tiled=True
        )
        act_value, act_slope = gelu_pair(part_act[0] + part_act[1])
        pre_grad = (rows_cot * act_slope).astype(bf16)
        hidden_rows, pre_grad = lax.optimization_barrier((act_value.astype(bf16), pre_grad))
        pair_grad = lax.all_gather(pre_grad, "core", axis=0, tiled=True)

    with jax.named_scope("weight_grad"):
        part_w = jnp.dot(normed, pair_grad, preferred_element_type=f32).astype(bf16)
        part_w, pair_grad = lax.optimization_barrier((part_w, pair_grad))
        pair_w = lax.psum_scatter(part_w, "z", scatter_dimension=0, tiled=True)

    def rows_grad(pair_grad):
        part_x = lax.dot_general(weight, pair_grad, (((1,), (1,)), ((), ())), preferred_element_type=f32)
        part_x = part_x.astype(bf16)
        scaled = part_x.astype(f32) * gain[:, None]
        sums = jnp.stack([jnp.sum(scaled, axis=0), jnp.sum(scaled * normal_x, axis=0)])
        by_yl = part_x.reshape(2, blocks, YH, depth, rows).transpose(2, 0, 1, 3, 4)
        by_yl = by_yl.reshape(YL, blocks * depth, rows)
        extra = jnp.broadcast_to(pieces_of(sums)[None], (YL, PIECES, rows))
        got = lax.all_to_all(
            jnp.concatenate([by_yl, extra], axis=1), "yl", split_axis=0, concat_axis=0, tiled=True
        )
        sums = sums_of(got[:, -PIECES:])
        grad = jnp.sum(got[:, :-PIECES].astype(f32), axis=0).astype(bf16)
        grad = jnp.concatenate([grad, pieces_of(sums)], axis=0)
        by_core = jnp.stack([grad[:, :KMOST], grad[:, KMOST:]])
        got = lax.all_to_all(by_core, "core", split_axis=0, concat_axis=0, tiled=True)
        sums = sums_of(got[:, -PIECES:])
        grad = got[:, :-PIECES].reshape(CORE, blocks, depth, KMOST).transpose(1, 0, 2, 3)
        by_x = grad.reshape(X, col_width, KMOST)
        extra = jnp.broadcast_to(pieces_of(sums)[None], (X, PIECES, KMOST))
        got = lax.all_to_all(
            jnp.concatenate([by_x, extra], axis=1), "x", split_axis=0, concat_axis=0, tiled=True
        )
        sums = sums_of(got[:, -PIECES:])
        share_grad = jnp.sum(got[:, :-PIECES].astype(f32), axis=0)


        return sums, share_grad

    with jax.named_scope("rows_grad"):
        sums, share_grad = lax.cond(
            keep_count[0] > 0,
            rows_grad,
            lambda g: (jnp.zeros((2, KMOST), f32), jnp.zeros((col_width, KMOST), f32)),
            pair_grad,
        )

    with jax.named_scope("rows_out"):
        col_start = (lax.axis_index("yl") * X + lax.axis_index("x")) * col_width
        share_gain = lax.dynamic_slice_in_dim(ln_gain, col_start, col_width, 0)
        own_mean = lax.dynamic_slice_in_dim(row_mean, core * KMOST, KMOST, 0)
        own_inv = lax.dynamic_slice_in_dim(inv_std, core * KMOST, KMOST, 0)
        share_x = (own_x.astype(f32) - own_mean[None, :]) * own_inv[None, :]
        scaled = share_grad * share_gain[:, None]
        means = sums / width
        grad_rows = own_inv[None, :] * (scaled - means[0:1] - share_x * means[1:2])
        grad_patches = lax.dot_general(
            select, grad_rows.astype(bf16), (((0,), (1,)), ((), ())), preferred_element_type=f32
        ).astype(bf16)
        hidden = lax.dot_general(
            select, hidden_rows, (((0,), (0,)), ((), ())), preferred_element_type=f32
        ).astype(bf16)

    with jax.named_scope("weight_out"):
        yh = lax.axis_index("yh")
        kept_w = lax.dynamic_slice_in_dim(pair_w, yh * depth, depth, 0)
        sent_w = lax.dynamic_slice_in_dim(pair_w, (1 - yh) * depth, depth, 0)
        met_w = lax.ppermute(sent_w, "yh", [(0, 1), (1, 0)])
        w_grad = kept_w.astype(f32) + met_w.astype(f32)
    return (hidden, grad_patches, w_grad)


def solution(mesh):
    fine = Mesh(mesh.devices.reshape(YH, Z, CORE, YL, X), ("yh", "z", "core", "yl", "x"))
    dp, tensor = ("yh", "z", "core"), ("yl", "x")
    both = P(dp, tensor)
    return jax.shard_map(
        per_device,
        mesh=fine,
        in_specs=(both, P(dp, None), P(dp), P(), both, both),
        out_specs=(both, both, both),
        check_vma=False,
    )
```

```python
import jax
import jax.numpy as jnp
from jax import lax
from jax.experimental import pallas as pl
from jax.experimental.pallas import tpu as pltpu
from jax.sharding import Mesh, PartitionSpec as P

KMOST = 192
YH, Z, CORE, YL, X = 2, 12, 2, 4, 4
PIECES = 16


def gelu_pair(pre_act):
    normal_cdf = 0.5 * (1.0 + lax.erf(pre_act * 0.7071067811865476))
    density = jnp.exp(-0.5 * pre_act * pre_act) * 0.3989422804014327
    return (pre_act * normal_cdf, normal_cdf + pre_act * density)


def pieces_of(sums):
    high = lax.reduce_precision(sums, 8, 7)
    rest = sums - high
    middle = lax.reduce_precision(rest, 8, 7)
    low = rest - middle
    parts = jnp.concatenate([high, middle, low], axis=-2).astype(jnp.bfloat16)
    pad = [(0, 0)] * (sums.ndim - 2) + [(0, PIECES - 6), (0, 0)]
    return jnp.pad(parts, pad)


def sums_of(parts):
    total = jnp.sum(parts[:, :6].astype(jnp.float32), axis=0)
    return total[0:2] + total[2:4] + total[4:6]


def columns_product(left, right):
    depth, rows = left.shape
    columns = right.shape[1]
    step = depth // 4

    def kernel(left_ref, right_ref, out_ref):
        product = lax.dot_general(
            left_ref[...], right_ref[...], (((0,), (0,)), ((), ())), preferred_element_type=jnp.float32
        )
        first = pl.program_id(0) == 0

        @pl.when(first)
        def _():
            out_ref[...] = product

        @pl.when(jnp.logical_not(first))
        def _():
            out_ref[...] += product

    return pl.pallas_call(
        kernel,
        out_shape=jax.ShapeDtypeStruct((rows, columns), jnp.float32),
        grid=(4,),
        in_specs=[pl.BlockSpec((step, rows), lambda i: (i, 0)), pl.BlockSpec((step, columns), lambda i: (i, 0))],
        out_specs=pl.BlockSpec((rows, columns), lambda i: (0, 0)),
        compiler_params=pltpu.CompilerParams(vmem_limit_bytes=24 << 20),
        name="columns_product",
    )(left, right)


def rows_product(left, right):
    rows, depth = left.shape
    columns = right.shape[1]
    step = rows // 4

    def kernel(left_ref, right_ref, out_ref):
        out_ref[...] = jnp.dot(left_ref[...], right_ref[...], preferred_element_type=jnp.float32).astype(out_ref.dtype)

    return pl.pallas_call(
        kernel,
        out_shape=jax.ShapeDtypeStruct((rows, columns), jnp.bfloat16),
        grid=(4,),
        in_specs=[pl.BlockSpec((step, depth), lambda i: (i, 0)), pl.BlockSpec((depth, columns), lambda i: (0, 0))],
        out_specs=pl.BlockSpec((step, columns), lambda i: (i, 0)),
        name="rows_product",
    )(left, right)


def per_device(patches, keep_order, keep_count, ln_gain, w_in, cotangent):
    own_rows, col_width = patches.shape
    depth, ff_width = w_in.shape
    width = ln_gain.shape[0]
    half = width // CORE
    core = lax.axis_index("core")
    bf16, f32 = jnp.bfloat16, jnp.float32

    slot_ids = jnp.arange(KMOST, dtype=jnp.int32)
    row_ids = jnp.arange(own_rows, dtype=jnp.int32)
    slot_row = jnp.where(slot_ids < keep_count[0], keep_order[0, :KMOST], -1)
    select = (slot_row[:, None] == row_ids[None, :]).astype(bf16)

    with jax.named_scope("weight_gather"):
        pair_weight = lax.all_gather(w_in, "yh", axis=0, tiled=True)
        weight = lax.all_gather(pair_weight, "z", axis=0, tiled=True)

    with jax.named_scope("own_rows"):
        own_x = lax.dot_general(
            patches, select, (((0,), (1,)), ((), ())), preferred_element_type=f32
        ).astype(bf16)

    with jax.named_scope("rows_gather"):
        block_x = lax.all_gather(own_x, "x", axis=0, tiled=True)
        blocks = block_x.shape[0] // (CORE * depth)
        by_core = block_x.reshape(blocks, CORE, depth, KMOST).transpose(1, 0, 2, 3)
        pair_x = lax.all_to_all(
            by_core.reshape(CORE, blocks * depth, KMOST), "core", split_axis=0, concat_axis=0, tiled=True
        )
        pair_x = jnp.concatenate([pair_x[0], pair_x[1]], axis=1)
        rows = pair_x.shape[1]
        cut = pair_x.shape[0] // 2
        parts = [lax.all_gather(pair_x[i * cut : (i + 1) * cut], "yl", axis=0, tiled=True) for i in range(2)]
        row_x = jnp.stack([p.reshape(YH, 2, blocks // 2, depth, rows) for p in parts])
        row_x = lax.optimization_barrier(row_x.transpose(2, 0, 3, 1, 4, 5).reshape(half, rows))

    with jax.named_scope("row_moments"):
        x32 = row_x.astype(f32)
        part_mean = jnp.mean(x32, axis=0)
        part_square = jnp.sum(jnp.square(x32 - part_mean[None, :]), axis=0)
        both = lax.all_gather(jnp.stack([part_mean, part_square]), "core", axis=0)
        row_mean = 0.5 * (both[0, 0] + both[1, 0])
        apart = both[0, 0] - both[1, 0]
        row_var = (both[0, 1] + both[1, 1] + apart * apart * (0.5 * half)) / width
        inv_std = lax.rsqrt(row_var + 1e-06)
        gain = ln_gain.reshape(YH, Z, CORE, depth)
        gain = lax.dynamic_index_in_dim(gain, core, 2, keepdims=False)
        gain = gain.transpose(1, 0, 2).reshape(half)
        normal_x = (x32 - row_mean[None, :]) * inv_std[None, :]
        normed = (normal_x * gain[:, None]).astype(bf16)

    with jax.named_scope("forward"):
        rows_cot = jnp.dot(select, cotangent, preferred_element_type=f32)
        part_act = columns_product(normed, weight)
        part_act = lax.all_to_all(
            part_act.reshape(CORE, KMOST, ff_width), "core", split_axis=0, concat_axis=0, tiled=True
        )
        act_value, act_slope = gelu_pair(part_act[0] + part_act[1])
        pre_grad = (rows_cot * act_slope).astype(bf16)
        hidden_rows, pre_grad = lax.optimization_barrier((act_value.astype(bf16), pre_grad))
        pair_grad = lax.all_gather(pre_grad, "core", axis=0, tiled=True)

    with jax.named_scope("weight_grad"):
        part_w = rows_product(normed, pair_grad)
        part_w, pair_grad = lax.optimization_barrier((part_w, pair_grad))
        pair_w = lax.psum_scatter(part_w, "z", scatter_dimension=0, tiled=True)

    def rows_grad(pair_grad, hidden_rows):
        hidden = lax.dot_general(
            select, hidden_rows, (((0,), (0,)), ((), ())), preferred_element_type=f32
        ).astype(bf16)
        part_x = lax.dot_general(weight, pair_grad, (((1,), (1,)), ((), ())), preferred_element_type=f32)
        part_x = part_x.astype(bf16)
        scaled = part_x.astype(f32) * gain[:, None]
        own_normal = (row_x.astype(f32) - row_mean[None, :]) * inv_std[None, :]
        sums = jnp.stack([jnp.sum(scaled, axis=0), jnp.sum(scaled * own_normal, axis=0)])
        by_yl = part_x.reshape(2, blocks, YH, depth, rows).transpose(2, 0, 1, 3, 4)
        by_yl = by_yl.reshape(YL, blocks * depth, rows)
        extra = jnp.broadcast_to(pieces_of(sums)[None], (YL, PIECES, rows))
        got = lax.all_to_all(
            jnp.concatenate([by_yl, extra], axis=1), "yl", split_axis=0, concat_axis=0, tiled=True
        )
        sums = sums_of(got[:, -PIECES:])
        grad = jnp.sum(got[:, :-PIECES].astype(f32), axis=0).astype(bf16)
        grad = jnp.concatenate([grad, pieces_of(sums)], axis=0)
        by_core = jnp.stack([grad[:, :KMOST], grad[:, KMOST:]])
        got = lax.all_to_all(by_core, "core", split_axis=0, concat_axis=0, tiled=True)
        sums = sums_of(got[:, -PIECES:])
        grad = got[:, :-PIECES].reshape(CORE, blocks, depth, KMOST).transpose(1, 0, 2, 3)
        by_x = grad.reshape(X, col_width, KMOST)
        extra = jnp.broadcast_to(pieces_of(sums)[None], (X, PIECES, KMOST))
        got = lax.all_to_all(
            jnp.concatenate([by_x, extra], axis=1), "x", split_axis=0, concat_axis=0, tiled=True
        )
        sums = sums_of(got[:, -PIECES:])
        share_grad = jnp.sum(got[:, :-PIECES].astype(f32), axis=0)


        return sums, share_grad, hidden

    def no_rows_grad(pair_grad, hidden_rows):
        return (
            jnp.zeros((2, KMOST), f32),
            jnp.zeros((col_width, KMOST), f32),
            jnp.zeros((own_rows, ff_width), bf16),
        )

    with jax.named_scope("rows_grad"):
        sums, share_grad, hidden = lax.cond(
            keep_count[0] > 0,
            rows_grad,
            no_rows_grad,
            pair_grad,
            hidden_rows,
        )

    with jax.named_scope("rows_out"):
        col_start = (lax.axis_index("yl") * X + lax.axis_index("x")) * col_width
        share_gain = lax.dynamic_slice_in_dim(ln_gain, col_start, col_width, 0)
        own_mean = lax.dynamic_slice_in_dim(row_mean, core * KMOST, KMOST, 0)
        own_inv = lax.dynamic_slice_in_dim(inv_std, core * KMOST, KMOST, 0)
        share_x = (own_x.astype(f32) - own_mean[None, :]) * own_inv[None, :]
        scaled = share_grad * share_gain[:, None]
        means = sums / width
        grad_rows = own_inv[None, :] * (scaled - means[0:1] - share_x * means[1:2])
        grad_patches = lax.dot_general(
            select, grad_rows.astype(bf16), (((0,), (1,)), ((), ())), preferred_element_type=f32
        ).astype(bf16)

    with jax.named_scope("weight_out"):
        yh = lax.axis_index("yh")
        kept_w = lax.dynamic_slice_in_dim(pair_w, yh * depth, depth, 0)
        sent_w = lax.dynamic_slice_in_dim(pair_w, (1 - yh) * depth, depth, 0)
        met_w = lax.ppermute(sent_w, "yh", [(0, 1), (1, 0)])
        w_grad = kept_w.astype(f32) + met_w.astype(f32)
    return (hidden, grad_patches, w_grad)


def solution(mesh):
    fine = Mesh(mesh.devices.reshape(YH, Z, CORE, YL, X), ("yh", "z", "core", "yl", "x"))
    dp, tensor = ("yh", "z", "core"), ("yl", "x")
    both = P(dp, tensor)
    return jax.shard_map(
        per_device,
        mesh=fine,
        in_specs=(both, P(dp, None), P(dp), P(), both, both),
        out_specs=(both, both, both),
        check_vma=False,
    )
```

```python
import jax
import jax.numpy as jnp
from jax import lax
from jax.sharding import Mesh, PartitionSpec as P

KMOST = 192
YH, Z, CORE, YL, X = 2, 12, 2, 4, 4
PIECES = 16


def gelu_pair(pre_act):
    normal_cdf = 0.5 * (1.0 + lax.erf(pre_act * 0.7071067811865476))
    density = jnp.exp(-0.5 * pre_act * pre_act) * 0.3989422804014327
    return (pre_act * normal_cdf, normal_cdf + pre_act * density)


def pieces_of(sums):
    high = lax.reduce_precision(sums, 8, 7)
    rest = sums - high
    middle = lax.reduce_precision(rest, 8, 7)
    low = rest - middle
    parts = jnp.concatenate([high, middle, low], axis=-2).astype(jnp.bfloat16)
    pad = [(0, 0)] * (sums.ndim - 2) + [(0, PIECES - 6), (0, 0)]
    return jnp.pad(parts, pad)


def sums_of(parts):
    total = jnp.sum(parts[:, :6].astype(jnp.float32), axis=0)
    return total[0:2] + total[2:4] + total[4:6]


def per_device(patches, keep_order, keep_count, ln_gain, w_in, cotangent):
    own_rows, col_width = patches.shape
    depth, ff_width = w_in.shape
    width = ln_gain.shape[0]
    half = width // CORE
    core = lax.axis_index("core")
    bf16, f32 = jnp.bfloat16, jnp.float32

    slot_ids = jnp.arange(KMOST, dtype=jnp.int32)
    row_ids = jnp.arange(own_rows, dtype=jnp.int32)
    slot_row = jnp.where(slot_ids < keep_count[0], keep_order[0, :KMOST], -1)
    select = (slot_row[:, None] == row_ids[None, :]).astype(bf16)

    with jax.named_scope("weight_gather"):
        pair_weight = lax.all_gather(w_in, "yh", axis=0, tiled=True)
        weight = lax.all_gather(pair_weight, "z", axis=0, tiled=True)

    with jax.named_scope("own_rows"):
        own_x = lax.dot_general(
            patches, select, (((0,), (1,)), ((), ())), preferred_element_type=f32
        ).astype(bf16)

    with jax.named_scope("rows_gather"):
        block_x = lax.all_gather(own_x, "x", axis=0, tiled=True)
        blocks = block_x.shape[0] // (CORE * depth)
        by_core = block_x.reshape(blocks, CORE, depth, KMOST).transpose(1, 0, 2, 3)
        pair_x = lax.all_to_all(
            by_core.reshape(CORE, blocks * depth, KMOST), "core", split_axis=0, concat_axis=0, tiled=True
        )
        pair_x = jnp.concatenate([pair_x[0], pair_x[1]], axis=1)
        rows = pair_x.shape[1]
        cut = pair_x.shape[0] // 2
        parts = [lax.all_gather(pair_x[i * cut : (i + 1) * cut], "yl", axis=0, tiled=True) for i in range(2)]
        row_x = jnp.stack([p.reshape(YH, 2, blocks // 2, depth, rows) for p in parts])
        row_x = lax.optimization_barrier(row_x.transpose(2, 0, 3, 1, 4, 5).reshape(half, rows))

    with jax.named_scope("row_moments"):
        x32 = row_x.astype(f32)
        part_mean = jnp.mean(x32, axis=0)
        part_square = jnp.sum(jnp.square(x32 - part_mean[None, :]), axis=0)
        both = lax.all_gather(jnp.stack([part_mean, part_square]), "core", axis=0)
        row_mean = 0.5 * (both[0, 0] + both[1, 0])
        apart = both[0, 0] - both[1, 0]
        row_var = (both[0, 1] + both[1, 1] + apart * apart * (0.5 * half)) / width
        inv_std = lax.rsqrt(row_var + 1e-06)
        gain = ln_gain.reshape(YH, Z, CORE, depth)
        gain = lax.dynamic_index_in_dim(gain, core, 2, keepdims=False)
        gain = gain.transpose(1, 0, 2).reshape(half)
        normal_x = (x32 - row_mean[None, :]) * inv_std[None, :]
        normed = lax.optimization_barrier((normal_x * gain[:, None]).astype(bf16))

    with jax.named_scope("forward"):
        rows_cot = jnp.dot(select, cotangent, preferred_element_type=f32)
        part_act = lax.dot_general(normed, weight, (((0,), (0,)), ((), ())), preferred_element_type=f32)
        part_act = lax.all_to_all(
            part_act.reshape(CORE, KMOST, ff_width), "core", split_axis=0, concat_axis=0, tiled=True
        )
        act_value, act_slope = gelu_pair(part_act[0] + part_act[1])
        pre_grad = (rows_cot * act_slope).astype(bf16)
        hidden_rows, pre_grad = lax.optimization_barrier((act_value.astype(bf16), pre_grad))
        pair_grad = lax.all_gather(pre_grad, "core", axis=0, tiled=True)

    with jax.named_scope("weight_grad"):
        part_w = jnp.dot(normed, pair_grad, preferred_element_type=f32).astype(bf16)
        part_w, pair_grad = lax.optimization_barrier((part_w, pair_grad))
        pair_w = lax.psum_scatter(part_w, "z", scatter_dimension=0, tiled=True)

    def rows_grad(pair_grad, hidden_rows):
        hidden = lax.dot_general(
            select, hidden_rows, (((0,), (0,)), ((), ())), preferred_element_type=f32
        ).astype(bf16)
        part_x = lax.dot_general(weight, pair_grad, (((1,), (1,)), ((), ())), preferred_element_type=f32)
        part_x = part_x.astype(bf16)
        scaled = part_x.astype(f32) * gain[:, None]
        own_normal = (row_x.astype(f32) - row_mean[None, :]) * inv_std[None, :]
        sums = jnp.stack([jnp.sum(scaled, axis=0), jnp.sum(scaled * own_normal, axis=0)])
        by_yl = part_x.reshape(2, blocks, YH, depth, rows).transpose(2, 0, 1, 3, 4)
        by_yl = by_yl.reshape(YL, blocks * depth, rows)
        extra = jnp.broadcast_to(pieces_of(sums)[None], (YL, PIECES, rows))
        got = lax.all_to_all(
            jnp.concatenate([by_yl, extra], axis=1), "yl", split_axis=0, concat_axis=0, tiled=True
        )
        sums = sums_of(got[:, -PIECES:])
        grad = jnp.sum(got[:, :-PIECES].astype(f32), axis=0).astype(bf16)
        grad = jnp.concatenate([grad, pieces_of(sums)], axis=0)
        by_core = jnp.stack([grad[:, :KMOST], grad[:, KMOST:]])
        got = lax.all_to_all(by_core, "core", split_axis=0, concat_axis=0, tiled=True)
        sums = sums_of(got[:, -PIECES:])
        grad = got[:, :-PIECES].reshape(CORE, blocks, depth, KMOST).transpose(1, 0, 2, 3)
        by_x = grad.reshape(X, col_width, KMOST)
        extra = jnp.broadcast_to(pieces_of(sums)[None], (X, PIECES, KMOST))
        got = lax.all_to_all(
            jnp.concatenate([by_x, extra], axis=1), "x", split_axis=0, concat_axis=0, tiled=True
        )
        sums = sums_of(got[:, -PIECES:])
        share_grad = jnp.sum(got[:, :-PIECES].astype(f32), axis=0)


        return sums, share_grad, hidden

    def no_rows_grad(pair_grad, hidden_rows):
        return (
            jnp.zeros((2, KMOST), f32),
            jnp.zeros((col_width, KMOST), f32),
            jnp.zeros((own_rows, ff_width), bf16),
        )

    with jax.named_scope("rows_grad"):
        sums, share_grad, hidden = lax.cond(
            keep_count[0] > 0,
            rows_grad,
            no_rows_grad,
            pair_grad,
            hidden_rows,
        )

    with jax.named_scope("rows_out"):
        col_start = (lax.axis_index("yl") * X + lax.axis_index("x")) * col_width
        share_gain = lax.dynamic_slice_in_dim(ln_gain, col_start, col_width, 0)
        own_mean = lax.dynamic_slice_in_dim(row_mean, core * KMOST, KMOST, 0)
        own_inv = lax.dynamic_slice_in_dim(inv_std, core * KMOST, KMOST, 0)
        share_x = (own_x.astype(f32) - own_mean[None, :]) * own_inv[None, :]
        scaled = share_grad * share_gain[:, None]
        means = sums / width
        grad_rows = own_inv[None, :] * (scaled - means[0:1] - share_x * means[1:2])
        grad_patches = lax.dot_general(
            select, grad_rows.astype(bf16), (((0,), (1,)), ((), ())), preferred_element_type=f32
        ).astype(bf16)

    with jax.named_scope("weight_out"):
        met_w = lax.all_to_all(pair_w.reshape(YH, depth, ff_width), "yh", split_axis=0, concat_axis=0, tiled=True)
        w_grad = met_w[0].astype(f32) + met_w[1].astype(f32)
    return (hidden, grad_patches, w_grad)


def solution(mesh):
    fine = Mesh(mesh.devices.reshape(YH, Z, CORE, YL, X), ("yh", "z", "core", "yl", "x"))
    dp, tensor = ("yh", "z", "core"), ("yl", "x")
    both = P(dp, tensor)
    return jax.shard_map(
        per_device,
        mesh=fine,
        in_specs=(both, P(dp, None), P(dp), P(), both, both),
        out_specs=(both, both, both),
        check_vma=False,
    )
```

```python
import jax
import jax.numpy as jnp
from jax import lax
from jax.sharding import Mesh, PartitionSpec as P

KMOST = 192
YH, Z, CORE, YL, X = 2, 12, 2, 4, 4
PIECES = 16


def gelu_pair(pre_act):
    normal_cdf = 0.5 * (1.0 + lax.erf(pre_act * 0.7071067811865476))
    density = jnp.exp(-0.5 * pre_act * pre_act) * 0.3989422804014327
    return (pre_act * normal_cdf, normal_cdf + pre_act * density)


def pieces_of(sums):
    high = lax.reduce_precision(sums, 8, 7)
    rest = sums - high
    middle = lax.reduce_precision(rest, 8, 7)
    low = rest - middle
    parts = jnp.concatenate([high, middle, low], axis=-2).astype(jnp.bfloat16)
    pad = [(0, 0)] * (sums.ndim - 2) + [(0, PIECES - 6), (0, 0)]
    return jnp.pad(parts, pad)


def sums_of(parts):
    total = jnp.sum(parts[:, :6].astype(jnp.float32), axis=0)
    return total[0:2] + total[2:4] + total[4:6]


def per_device(patches, keep_order, keep_count, ln_gain, w_in, cotangent):
    own_rows, col_width = patches.shape
    depth, ff_width = w_in.shape
    width = ln_gain.shape[0]
    half = width // CORE
    core = lax.axis_index("core")
    bf16, f32 = jnp.bfloat16, jnp.float32

    slot_ids = jnp.arange(KMOST, dtype=jnp.int32)
    row_ids = jnp.arange(own_rows, dtype=jnp.int32)
    slot_row = jnp.where(slot_ids < keep_count[0], keep_order[0, :KMOST], -1)
    select = (slot_row[:, None] == row_ids[None, :]).astype(bf16)

    with jax.named_scope("weight_gather"):
        pair_weight = lax.all_gather(w_in, "yh", axis=0, tiled=True)
        weight = lax.all_gather(pair_weight, "z", axis=0, tiled=True)

    with jax.named_scope("own_rows"):
        own_x = lax.dot_general(
            patches, select, (((0,), (1,)), ((), ())), preferred_element_type=f32
        ).astype(bf16)

    with jax.named_scope("rows_gather"):
        block_x = lax.all_gather(own_x, "x", axis=0, tiled=True)
        blocks = block_x.shape[0] // (CORE * depth)
        by_core = block_x.reshape(blocks, CORE, depth, KMOST).transpose(1, 0, 2, 3)
        pair_x = lax.all_to_all(
            by_core.reshape(CORE, blocks * depth, KMOST), "core", split_axis=0, concat_axis=0, tiled=True
        )
        pair_x = jnp.concatenate([pair_x[0], pair_x[1]], axis=1)
        rows = pair_x.shape[1]
        cut = pair_x.shape[0] // 2
        parts = [lax.all_gather(pair_x[i * cut : (i + 1) * cut], "yl", axis=0, tiled=True) for i in range(2)]
        row_x = jnp.stack([p.reshape(YH, 2, blocks // 2, depth, rows) for p in parts])
        row_x = lax.optimization_barrier(row_x.transpose(2, 0, 3, 1, 4, 5).reshape(half, rows))

    with jax.named_scope("row_moments"):
        x32 = row_x.astype(f32)
        part_mean = jnp.mean(x32, axis=0)
        part_square = jnp.sum(jnp.square(x32 - part_mean[None, :]), axis=0)
        both = lax.all_gather(jnp.stack([part_mean, part_square]), "core", axis=0)
        row_mean = 0.5 * (both[0, 0] + both[1, 0])
        apart = both[0, 0] - both[1, 0]
        row_var = (both[0, 1] + both[1, 1] + apart * apart * (0.5 * half)) / width
        inv_std = lax.rsqrt(row_var + 1e-06)
        gain = ln_gain.reshape(YH, Z, CORE, depth)
        gain = lax.dynamic_index_in_dim(gain, core, 2, keepdims=False)
        gain = gain.transpose(1, 0, 2).reshape(half)
        normal_x = (x32 - row_mean[None, :]) * inv_std[None, :]
        normed = lax.optimization_barrier((normal_x * gain[:, None]).astype(bf16))

    with jax.named_scope("forward"):
        rows_cot = jnp.dot(select, cotangent, preferred_element_type=f32)
        part_act = lax.dot_general(normed, weight, (((0,), (0,)), ((), ())), preferred_element_type=f32)
        part_act = lax.all_to_all(
            part_act.reshape(CORE, KMOST, ff_width), "core", split_axis=0, concat_axis=0, tiled=True
        )
        act_value, act_slope = gelu_pair(part_act[0] + part_act[1])
        pre_grad = (rows_cot * act_slope).astype(bf16)
        hidden_rows, pre_grad = lax.optimization_barrier((act_value.astype(bf16), pre_grad))
        pair_grad = lax.all_gather(pre_grad, "core", axis=0, tiled=True)

    with jax.named_scope("weight_grad"):
        part_w = jnp.dot(normed, pair_grad, preferred_element_type=f32).astype(bf16)
        pair_w = lax.psum_scatter(part_w, "z", scatter_dimension=0, tiled=True)

    def rows_grad(pair_grad, hidden_rows):
        hidden = lax.dot_general(
            select, hidden_rows, (((0,), (0,)), ((), ())), preferred_element_type=f32
        ).astype(bf16)
        part_x = lax.dot_general(weight, pair_grad, (((1,), (1,)), ((), ())), preferred_element_type=f32)
        part_x = part_x.astype(bf16)
        scaled = part_x.astype(f32) * gain[:, None]
        own_normal = (row_x.astype(f32) - row_mean[None, :]) * inv_std[None, :]
        sums = jnp.stack([jnp.sum(scaled, axis=0), jnp.sum(scaled * own_normal, axis=0)])
        by_yl = part_x.reshape(2, blocks, YH, depth, rows).transpose(2, 0, 1, 3, 4)
        by_yl = by_yl.reshape(YL, blocks * depth, rows)
        extra = jnp.broadcast_to(pieces_of(sums)[None], (YL, PIECES, rows))
        got = lax.all_to_all(
            jnp.concatenate([by_yl, extra], axis=1), "yl", split_axis=0, concat_axis=0, tiled=True
        )
        sums = sums_of(got[:, -PIECES:])
        grad = jnp.sum(got[:, :-PIECES].astype(f32), axis=0).astype(bf16)
        grad = jnp.concatenate([grad, pieces_of(sums)], axis=0)
        by_core = jnp.stack([grad[:, :KMOST], grad[:, KMOST:]])
        got = lax.all_to_all(by_core, "core", split_axis=0, concat_axis=0, tiled=True)
        sums = sums_of(got[:, -PIECES:])
        grad = got[:, :-PIECES].reshape(CORE, blocks, depth, KMOST).transpose(1, 0, 2, 3)
        by_x = grad.reshape(X, col_width, KMOST)
        extra = jnp.broadcast_to(pieces_of(sums)[None], (X, PIECES, KMOST))
        got = lax.all_to_all(
            jnp.concatenate([by_x, extra], axis=1), "x", split_axis=0, concat_axis=0, tiled=True
        )
        sums = sums_of(got[:, -PIECES:])
        share_grad = jnp.sum(got[:, :-PIECES].astype(f32), axis=0)


        return sums, share_grad, hidden

    def no_rows_grad(pair_grad, hidden_rows):
        return (
            jnp.zeros((2, KMOST), f32),
            jnp.zeros((col_width, KMOST), f32),
            jnp.zeros((own_rows, ff_width), bf16),
        )

    with jax.named_scope("rows_grad"):
        sums, share_grad, hidden = lax.cond(
            keep_count[0] > 0,
            rows_grad,
            no_rows_grad,
            pair_grad,
            hidden_rows,
        )

    with jax.named_scope("rows_out"):
        col_start = (lax.axis_index("yl") * X + lax.axis_index("x")) * col_width
        share_gain = lax.dynamic_slice_in_dim(ln_gain, col_start, col_width, 0)
        own_mean = lax.dynamic_slice_in_dim(row_mean, core * KMOST, KMOST, 0)
        own_inv = lax.dynamic_slice_in_dim(inv_std, core * KMOST, KMOST, 0)
        share_x = (own_x.astype(f32) - own_mean[None, :]) * own_inv[None, :]
        scaled = share_grad * share_gain[:, None]
        means = sums / width
        grad_rows = own_inv[None, :] * (scaled - means[0:1] - share_x * means[1:2])
        grad_patches = lax.dot_general(
            select, grad_rows.astype(bf16), (((0,), (1,)), ((), ())), preferred_element_type=f32
        ).astype(bf16)

    with jax.named_scope("weight_out"):
        yh = lax.axis_index("yh")
        kept_w = lax.dynamic_slice_in_dim(pair_w, yh * depth, depth, 0)
        sent_w = lax.dynamic_slice_in_dim(pair_w, (1 - yh) * depth, depth, 0)
        met_w = lax.ppermute(sent_w, "yh", [(0, 1), (1, 0)])
        w_grad = kept_w.astype(f32) + met_w.astype(f32)
    return (hidden, grad_patches, w_grad)


def solution(mesh):
    fine = Mesh(mesh.devices.reshape(YH, Z, CORE, YL, X), ("yh", "z", "core", "yl", "x"))
    dp, tensor = ("yh", "z", "core"), ("yl", "x")
    both = P(dp, tensor)
    return jax.shard_map(
        per_device,
        mesh=fine,
        in_specs=(both, P(dp, None), P(dp), P(), both, both),
        out_specs=(both, both, both),
        check_vma=False,
    )
```

```python
import jax
import jax.numpy as jnp
from jax import lax
from jax.sharding import Mesh, PartitionSpec as P

KMOST = 192
YH, Z, CORE, YL, X = 2, 12, 2, 4, 4
PIECES = 16


def gelu_pair(pre_act):
    normal_cdf = 0.5 * (1.0 + lax.erf(pre_act * 0.7071067811865476))
    density = jnp.exp(-0.5 * pre_act * pre_act) * 0.3989422804014327
    return (pre_act * normal_cdf, normal_cdf + pre_act * density)


def pieces_of(sums):
    high = lax.reduce_precision(sums, 8, 7)
    rest = sums - high
    middle = lax.reduce_precision(rest, 8, 7)
    low = rest - middle
    parts = jnp.concatenate([high, middle, low], axis=-2).astype(jnp.bfloat16)
    pad = [(0, 0)] * (sums.ndim - 2) + [(0, PIECES - 6), (0, 0)]
    return jnp.pad(parts, pad)


def sums_of(parts):
    total = jnp.sum(parts[:, :6].astype(jnp.float32), axis=0)
    return total[0:2] + total[2:4] + total[4:6]


def per_device(patches, keep_order, keep_count, ln_gain, w_in, cotangent):
    own_rows, col_width = patches.shape
    depth, ff_width = w_in.shape
    width = ln_gain.shape[0]
    half = width // CORE
    core = lax.axis_index("core")
    bf16, f32 = jnp.bfloat16, jnp.float32

    slot_ids = jnp.arange(KMOST, dtype=jnp.int32)
    row_ids = jnp.arange(own_rows, dtype=jnp.int32)
    slot_row = jnp.where(slot_ids < keep_count[0], keep_order[0, :KMOST], -1)
    select = (slot_row[:, None] == row_ids[None, :]).astype(bf16)

    with jax.named_scope("weight_gather"):
        pair_weight = lax.all_gather(w_in, "yh", axis=0, tiled=True)
        weight = lax.all_gather(pair_weight, "z", axis=0, tiled=True)

    with jax.named_scope("own_rows"):
        own_x = lax.dot_general(
            patches, select, (((0,), (1,)), ((), ())), preferred_element_type=f32
        ).astype(bf16)

    with jax.named_scope("rows_gather"):
        block_x = lax.all_gather(own_x, "x", axis=0, tiled=True)
        blocks = block_x.shape[0] // (CORE * depth)
        by_core = block_x.reshape(blocks, CORE, depth, KMOST).transpose(1, 0, 2, 3)
        pair_x = lax.all_to_all(
            by_core.reshape(CORE, blocks * depth, KMOST), "core", split_axis=0, concat_axis=0, tiled=True
        )
        pair_x = jnp.concatenate([pair_x[0], pair_x[1]], axis=1)
        rows = pair_x.shape[1]
        cut = pair_x.shape[0] // 2
        parts = [lax.all_gather(pair_x[i * cut : (i + 1) * cut], "yl", axis=0, tiled=True) for i in range(2)]
        row_x = jnp.stack([p.reshape(YH, 2, blocks // 2, depth, rows) for p in parts])
        row_x = lax.optimization_barrier(row_x.transpose(2, 0, 3, 1, 4, 5).reshape(half, rows))

    with jax.named_scope("row_moments"):
        x32 = row_x.astype(f32)
        part_mean = jnp.mean(x32, axis=0)
        part_square = jnp.sum(jnp.square(x32 - part_mean[None, :]), axis=0)
        both = lax.all_gather(jnp.stack([part_mean, part_square]), "core", axis=0)
        row_mean = 0.5 * (both[0, 0] + both[1, 0])
        apart = both[0, 0] - both[1, 0]
        row_var = (both[0, 1] + both[1, 1] + apart * apart * (0.5 * half)) / width
        inv_std = lax.rsqrt(row_var + 1e-06)
        gain = ln_gain.reshape(YH, Z, CORE, depth)
        gain = lax.dynamic_index_in_dim(gain, core, 2, keepdims=False)
        gain = gain.transpose(1, 0, 2).reshape(half)
        normal_x = (x32 - row_mean[None, :]) * inv_std[None, :]
        normed = lax.optimization_barrier((normal_x * gain[:, None]).astype(bf16))

    with jax.named_scope("forward"):
        rows_cot = jnp.dot(select, cotangent, preferred_element_type=f32)
        part_act = lax.dot_general(normed, weight, (((0,), (0,)), ((), ())), preferred_element_type=f32)
        part_act = lax.all_to_all(
            part_act.reshape(CORE, KMOST, ff_width), "core", split_axis=0, concat_axis=0, tiled=True
        )
        act_value, act_slope = gelu_pair(part_act[0] + part_act[1])
        pre_grad = (rows_cot * act_slope).astype(bf16)
        hidden_rows, pre_grad = lax.optimization_barrier((act_value.astype(bf16), pre_grad))
        pair_grad = lax.all_gather(pre_grad, "core", axis=0, tiled=True)

    with jax.named_scope("weight_grad"):
        part_w = jnp.dot(normed, pair_grad, preferred_element_type=f32).astype(bf16)
        pair_w = lax.psum_scatter(part_w, "z", scatter_dimension=0, tiled=True)

    def rows_grad(pair_grad, hidden_rows):
        hidden = lax.dot_general(
            select, hidden_rows, (((0,), (0,)), ((), ())), preferred_element_type=f32
        ).astype(bf16)
        part_x = lax.dot_general(weight, pair_grad, (((1,), (1,)), ((), ())), preferred_element_type=f32)
        part_x = part_x.astype(bf16)
        part_32 = part_x.astype(f32)
        sums = jnp.stack([jnp.sum(part_32 * gain[:, None], axis=0), jnp.sum(part_32 * normed.astype(f32), axis=0)])
        by_yl = part_x.reshape(2, blocks, YH, depth, rows).transpose(2, 0, 1, 3, 4)
        by_yl = by_yl.reshape(YL, blocks * depth, rows)
        extra = jnp.broadcast_to(pieces_of(sums)[None], (YL, PIECES, rows))
        got = lax.all_to_all(
            jnp.concatenate([by_yl, extra], axis=1), "yl", split_axis=0, concat_axis=0, tiled=True
        )
        sums = sums_of(got[:, -PIECES:])
        grad = jnp.sum(got[:, :-PIECES].astype(f32), axis=0).astype(bf16)
        grad = jnp.concatenate([grad, pieces_of(sums)], axis=0)
        by_core = jnp.stack([grad[:, :KMOST], grad[:, KMOST:]])
        got = lax.all_to_all(by_core, "core", split_axis=0, concat_axis=0, tiled=True)
        sums = sums_of(got[:, -PIECES:])
        grad = got[:, :-PIECES].reshape(CORE, blocks, depth, KMOST).transpose(1, 0, 2, 3)
        by_x = grad.reshape(X, col_width, KMOST)
        extra = jnp.broadcast_to(pieces_of(sums)[None], (X, PIECES, KMOST))
        got = lax.all_to_all(
            jnp.concatenate([by_x, extra], axis=1), "x", split_axis=0, concat_axis=0, tiled=True
        )
        sums = sums_of(got[:, -PIECES:])
        share_grad = jnp.sum(got[:, :-PIECES].astype(f32), axis=0)


        return sums, share_grad, hidden

    def no_rows_grad(pair_grad, hidden_rows):
        return (
            jnp.zeros((2, KMOST), f32),
            jnp.zeros((col_width, KMOST), f32),
            jnp.zeros((own_rows, ff_width), bf16),
        )

    with jax.named_scope("rows_grad"):
        sums, share_grad, hidden = lax.cond(
            keep_count[0] > 0,
            rows_grad,
            no_rows_grad,
            pair_grad,
            hidden_rows,
        )

    with jax.named_scope("rows_out"):
        col_start = (lax.axis_index("yl") * X + lax.axis_index("x")) * col_width
        share_gain = lax.dynamic_slice_in_dim(ln_gain, col_start, col_width, 0)
        own_mean = lax.dynamic_slice_in_dim(row_mean, core * KMOST, KMOST, 0)
        own_inv = lax.dynamic_slice_in_dim(inv_std, core * KMOST, KMOST, 0)
        share_x = (own_x.astype(f32) - own_mean[None, :]) * own_inv[None, :]
        scaled = share_grad * share_gain[:, None]
        means = sums / width
        grad_rows = own_inv[None, :] * (scaled - means[0:1] - share_x * means[1:2])
        grad_patches = lax.dot_general(
            select, grad_rows.astype(bf16), (((0,), (1,)), ((), ())), preferred_element_type=f32
        ).astype(bf16)

    with jax.named_scope("weight_out"):
        yh = lax.axis_index("yh")
        kept_w = lax.dynamic_slice_in_dim(pair_w, yh * depth, depth, 0)
        sent_w = lax.dynamic_slice_in_dim(pair_w, (1 - yh) * depth, depth, 0)
        kept_w, sent_w = lax.optimization_barrier((kept_w, sent_w))
        met_w = lax.ppermute(sent_w, "yh", [(0, 1), (1, 0)])
        w_grad = kept_w.astype(f32) + met_w.astype(f32)
    return (hidden, grad_patches, w_grad)


def solution(mesh):
    fine = Mesh(mesh.devices.reshape(YH, Z, CORE, YL, X), ("yh", "z", "core", "yl", "x"))
    dp, tensor = ("yh", "z", "core"), ("yl", "x")
    both = P(dp, tensor)
    return jax.shard_map(
        per_device,
        mesh=fine,
        in_specs=(both, P(dp, None), P(dp), P(), both, both),
        out_specs=(both, both, both),
        check_vma=False,
    )
```

```python
import jax
import jax.numpy as jnp
from jax import lax
from jax.sharding import Mesh, PartitionSpec as P

KMOST = 192
YH, Z, CORE, YL, X = 2, 12, 2, 4, 4
PIECES = 16


def gelu_pair(pre_act):
    normal_cdf = 0.5 * (1.0 + lax.erf(pre_act * 0.7071067811865476))
    density = jnp.exp(-0.5 * pre_act * pre_act) * 0.3989422804014327
    return (pre_act * normal_cdf, normal_cdf + pre_act * density)


def pieces_of(sums):
    high = lax.reduce_precision(sums, 8, 7)
    rest = sums - high
    middle = lax.reduce_precision(rest, 8, 7)
    low = rest - middle
    parts = jnp.concatenate([high, middle, low], axis=-2).astype(jnp.bfloat16)
    pad = [(0, 0)] * (sums.ndim - 2) + [(0, PIECES - 6), (0, 0)]
    return jnp.pad(parts, pad)


def sums_of(parts):
    total = jnp.sum(parts[:, :6].astype(jnp.float32), axis=0)
    return total[0:2] + total[2:4] + total[4:6]


def per_device(patches, keep_order, keep_count, ln_gain, w_in, cotangent):
    own_rows, col_width = patches.shape
    depth, ff_width = w_in.shape
    width = ln_gain.shape[0]
    half = width // CORE
    core = lax.axis_index("core")
    bf16, f32 = jnp.bfloat16, jnp.float32

    slot_ids = jnp.arange(KMOST, dtype=jnp.int32)
    row_ids = jnp.arange(own_rows, dtype=jnp.int32)
    slot_row = jnp.where(slot_ids < keep_count[0], keep_order[0, :KMOST], -1)
    select = (slot_row[:, None] == row_ids[None, :]).astype(bf16)

    with jax.named_scope("weight_gather"):
        pair_weight = lax.all_gather(w_in, "yh", axis=0, tiled=True)
        weight = lax.all_gather(pair_weight, "z", axis=0, tiled=True)

    with jax.named_scope("own_rows"):
        own_x = lax.dot_general(
            patches, select, (((0,), (1,)), ((), ())), preferred_element_type=f32
        ).astype(bf16)

    with jax.named_scope("rows_gather"):
        block_x = lax.all_gather(own_x, "x", axis=0, tiled=True)
        blocks = block_x.shape[0] // (CORE * depth)
        by_core = block_x.reshape(blocks, CORE, depth, KMOST).transpose(1, 0, 2, 3)
        pair_x = lax.all_to_all(
            by_core.reshape(CORE, blocks * depth, KMOST), "core", split_axis=0, concat_axis=0, tiled=True
        )
        pair_x = jnp.concatenate([pair_x[0], pair_x[1]], axis=1)
        rows = pair_x.shape[1]
        cut = pair_x.shape[0] // 2
        parts = [lax.all_gather(pair_x[i * cut : (i + 1) * cut], "yl", axis=0, tiled=True) for i in range(2)]
        row_x = jnp.stack([p.reshape(YH, 2, blocks // 2, depth, rows) for p in parts])
        row_x = lax.optimization_barrier(row_x.transpose(2, 0, 3, 1, 4, 5).reshape(half, rows))

    with jax.named_scope("row_moments"):
        x32 = row_x.astype(f32)
        part_mean = jnp.mean(x32, axis=0)
        part_square = jnp.sum(jnp.square(x32 - part_mean[None, :]), axis=0)
        both = lax.all_gather(jnp.stack([part_mean, part_square]), "core", axis=0)
        row_mean = 0.5 * (both[0, 0] + both[1, 0])
        apart = both[0, 0] - both[1, 0]
        row_var = (both[0, 1] + both[1, 1] + apart * apart * (0.5 * half)) / width
        inv_std = lax.rsqrt(row_var + 1e-06)
        gain = ln_gain.reshape(YH, Z, CORE, depth)
        gain = lax.dynamic_index_in_dim(gain, core, 2, keepdims=False)
        gain = gain.transpose(1, 0, 2).reshape(half)
        normal_x = (x32 - row_mean[None, :]) * inv_std[None, :]
        normed = lax.optimization_barrier((normal_x * gain[:, None]).astype(bf16))

    with jax.named_scope("forward"):
        rows_cot = jnp.dot(select, cotangent, preferred_element_type=f32)
        part_act = lax.dot_general(normed, weight, (((0,), (0,)), ((), ())), preferred_element_type=f32)
        low = core == 0
        sent_act = jnp.where(low, part_act[KMOST:], part_act[:KMOST]).astype(bf16)
        met_act = lax.all_gather(sent_act, "core", axis=0)
        own_act = jnp.where(low, part_act[:KMOST], part_act[KMOST:])
        met_act = jnp.where(low, met_act[1], met_act[0]).astype(f32)
        act_value, act_slope = gelu_pair(own_act + met_act)
        pre_grad = (rows_cot * act_slope).astype(bf16)
        hidden_rows, pre_grad = lax.optimization_barrier((act_value.astype(bf16), pre_grad))
        pair_grad = lax.all_gather(pre_grad, "core", axis=0, tiled=True)

    with jax.named_scope("weight_grad"):
        part_w = jnp.dot(normed, pair_grad, preferred_element_type=f32).astype(bf16)
        pair_w = lax.psum_scatter(part_w, "z", scatter_dimension=0, tiled=True)

    def rows_grad(pair_grad, hidden_rows):
        hidden = lax.dot_general(
            select, hidden_rows, (((0,), (0,)), ((), ())), preferred_element_type=f32
        ).astype(bf16)
        part_x = lax.dot_general(weight, pair_grad, (((1,), (1,)), ((), ())), preferred_element_type=f32)
        part_x = part_x.astype(bf16)
        part_32 = part_x.astype(f32)
        sums = jnp.stack([jnp.sum(part_32 * gain[:, None], axis=0), jnp.sum(part_32 * normed.astype(f32), axis=0)])
        by_yl = part_x.reshape(2, blocks, YH, depth, rows).transpose(2, 0, 1, 3, 4)
        by_yl = by_yl.reshape(YL, blocks * depth, rows)
        extra = jnp.broadcast_to(pieces_of(sums)[None], (YL, PIECES, rows))
        got = lax.all_to_all(
            jnp.concatenate([by_yl, extra], axis=1), "yl", split_axis=0, concat_axis=0, tiled=True
        )
        sums = sums_of(got[:, -PIECES:])
        grad = jnp.sum(got[:, :-PIECES].astype(f32), axis=0).astype(bf16)
        grad = jnp.concatenate([grad, pieces_of(sums)], axis=0)
        by_core = jnp.stack([grad[:, :KMOST], grad[:, KMOST:]])
        got = lax.all_to_all(by_core, "core", split_axis=0, concat_axis=0, tiled=True)
        sums = sums_of(got[:, -PIECES:])
        grad = got[:, :-PIECES].reshape(CORE, blocks, depth, KMOST).transpose(1, 0, 2, 3)
        by_x = grad.reshape(X, col_width, KMOST)
        extra = jnp.broadcast_to(pieces_of(sums)[None], (X, PIECES, KMOST))
        got = lax.all_to_all(
            jnp.concatenate([by_x, extra], axis=1), "x", split_axis=0, concat_axis=0, tiled=True
        )
        sums = sums_of(got[:, -PIECES:])
        share_grad = jnp.sum(got[:, :-PIECES].astype(f32), axis=0)


        return sums, share_grad, hidden

    def no_rows_grad(pair_grad, hidden_rows):
        return (
            jnp.zeros((2, KMOST), f32),
            jnp.zeros((col_width, KMOST), f32),
            jnp.zeros((own_rows, ff_width), bf16),
        )

    with jax.named_scope("rows_grad"):
        sums, share_grad, hidden = lax.cond(
            keep_count[0] > 0,
            rows_grad,
            no_rows_grad,
            pair_grad,
            hidden_rows,
        )

    with jax.named_scope("rows_out"):
        col_start = (lax.axis_index("yl") * X + lax.axis_index("x")) * col_width
        share_gain = lax.dynamic_slice_in_dim(ln_gain, col_start, col_width, 0)
        own_mean = lax.dynamic_slice_in_dim(row_mean, core * KMOST, KMOST, 0)
        own_inv = lax.dynamic_slice_in_dim(inv_std, core * KMOST, KMOST, 0)
        share_x = (own_x.astype(f32) - own_mean[None, :]) * own_inv[None, :]
        scaled = share_grad * share_gain[:, None]
        means = sums / width
        grad_rows = own_inv[None, :] * (scaled - means[0:1] - share_x * means[1:2])
        grad_patches = lax.dot_general(
            select, grad_rows.astype(bf16), (((0,), (1,)), ((), ())), preferred_element_type=f32
        ).astype(bf16)

    with jax.named_scope("weight_out"):
        yh = lax.axis_index("yh")
        kept_w = lax.dynamic_slice_in_dim(pair_w, yh * depth, depth, 0)
        sent_w = lax.dynamic_slice_in_dim(pair_w, (1 - yh) * depth, depth, 0)
        kept_w, sent_w = lax.optimization_barrier((kept_w, sent_w))
        met_w = lax.ppermute(sent_w, "yh", [(0, 1), (1, 0)])
        w_grad = kept_w.astype(f32) + met_w.astype(f32)
    return (hidden, grad_patches, w_grad)


def solution(mesh):
    fine = Mesh(mesh.devices.reshape(YH, Z, CORE, YL, X), ("yh", "z", "core", "yl", "x"))
    dp, tensor = ("yh", "z", "core"), ("yl", "x")
    both = P(dp, tensor)
    return jax.shard_map(
        per_device,
        mesh=fine,
        in_specs=(both, P(dp, None), P(dp), P(), both, both),
        out_specs=(both, both, both),
        check_vma=False,
    )
```
